32 devices in a mesh: prow: 8 (over y, x, core), pcol: 4 (over z).
Axes of the slice: x: 2, y: 2, z: 4, core: 2. Of those that a mesh axis runs over, the one named last changes fastest.
Arguments:
- block: float32 [16384, 5120], P('prow', 'pcol'), may hold values from -6 to 6
Outputs:
- top: float32 [256, 5120], P(None, 'pcol')
- updated: float32 [16384, 5120], P('prow', 'pcol')
The draws below stay inside these ranges and needn't reach their ends.
All inputs are finite; a program needn't handle non-finite values.
Results may differ from the reference program's by a relative error of at most 0.000073.
Values sent between devices are 32-bit elements; how exact they have to be, the bound alone decides.
A program may use at most 128 MiB of HBM per device.

```python
import jax
import jax.numpy as jnp
from jax import lax

NB = 256
MROWS = 16384
NCOL = 5120


def block_levels(stream_key, dims, shards, smallest, top_value):
    def one(dim, parts):
        steps = jax.random.uniform(jax.random.fold_in(jax.random.fold_in(stream_key, 6), dim), (parts,), jnp.float32, smallest / len(shards), top_value / len(shards))
        return jnp.repeat(jnp.exp(steps), dims[dim] // parts).reshape((-1,) + (1,) * (len(dims) - dim - 1))

    gain = one(*shards[0])
    for cut in shards[1:]:
        gain = gain * one(*cut)
    return gain


def centred(key, extent, scale, reach, shards=(), kind=jnp.bfloat16):
    gain = block_levels(key, extent, shards, -0.22, 0.18) if shards else 1.0
    result = jax.random.normal(key, extent, jnp.float32) * scale * gain
    return jnp.minimum(jnp.maximum(result, -reach), reach).astype(kind)


def setup_inputs(seed: int = 0) -> dict:
    keys = jax.random.split(jax.random.key(seed), 2)
    block = centred(keys[0], (MROWS, NCOL), 1.0, 6.0, ((0, 8), (1, 4)), jnp.float32)
    return dict(block=block)


def solve_triangular(matrix, right, lower):
    return jax.scipy.linalg.solve_triangular(matrix, right, lower=lower)

def reference(block):
    highest = lax.Precision.HIGHEST
    panel = block[:, :NB]
    gram = jnp.dot(panel.T.astype(jnp.float32), panel.astype(jnp.float32), precision=highest, preferred_element_type=jnp.float32)
    factor = jnp.linalg.cholesky(gram)
    products = jnp.dot(panel.T.astype(jnp.float32), block.astype(jnp.float32), precision=highest, preferred_element_type=jnp.float32)
    top = solve_triangular(factor, products, True)
    basis = solve_triangular(factor, panel.T, True).T
    rest = block[:, NB:] - jnp.dot(basis.astype(jnp.float32), top[:, NB:].astype(jnp.float32), precision=highest, preferred_element_type=jnp.float32)
    updated = jnp.concatenate([basis, rest], axis=1)
    return (top, updated)
```

```python
import functools

import jax
import jax.numpy as jnp
from jax import lax
from jax.experimental import pallas as pl
from jax.experimental.pallas import tpu as pltpu
from jax.sharding import PartitionSpec as P

NB = 256
HALF = 128
ROWS = 256
DIAG = 64
HIGHEST = lax.Precision.HIGHEST
F32 = jnp.float32


def split(x):
    hi = x.astype(jnp.bfloat16)
    return hi, (x - hi.astype(F32)).astype(jnp.bfloat16)


def dot3(a, b):
    dot = functools.partial(jnp.dot, preferred_element_type=F32)
    return dot(a[0], b[0]) + (dot(a[0], b[1]) + dot(a[1], b[0]))


def inverse_factor(square):
    n = square.shape[0]
    row_id = lax.broadcasted_iota(jnp.int32, (n, 1), 0)
    eye = (
        lax.broadcasted_iota(jnp.int32, (n, n), 0)
        == lax.broadcasted_iota(jnp.int32, (n, n), 1)
    ).astype(F32)
    m = jnp.concatenate([square, eye], axis=1)
    for k in range(n - 1):
        row = m[k : k + 1, :]
        scaled = row / row[:, k : k + 1]
        m = m - jnp.where(row_id > k, m[:, k : k + 1], 0.0) * scaled
    pivots = jnp.sum(m[:, :n] * eye, axis=1, keepdims=True)
    return m[:, n:] / jnp.sqrt(pivots)


def inverse_cholesky(work):
    for start in range(0, NB, DIAG):
        end = start + DIAG
        inv = inverse_factor(work[start:end, start:end])
        new = jnp.dot(inv, work[start:end, :], precision=HIGHEST, preferred_element_type=F32)
        work[start:end, :] = new
        if end < NB:
            turned = new[:, :NB].T
            work[end:, :] = work[end:, :] - jnp.dot(
                turned[end:, :], new, precision=HIGHEST, preferred_element_type=F32
            )


def gather_kernel(
    np_, nq, block, panel_out, linv_out, prod_out,
    blk, panel, acc, parts, prod, gram, gparts, gfull, work, linv,
    load_sem, blk_sem, csend, crecv, gsend, grecv, hsend, hrecv,
    psend, precv, asend, arecv, zsend, zrecv, lsend, lrecv, out_sem,
):
    p = lax.axis_index("prow")
    q = lax.axis_index("pcol")
    rows, cols = blk.shape
    steps = rows // ROWS
    chunks = 2 * steps
    first = q == 0
    inner = q > 0
    sends_on = q < nq - 1
    gs = NB // np_
    ps = HALF // np_

    def remote(src, dst, send, recv, pp, qq):
        return pltpu.make_async_remote_copy(
            src_ref=src, dst_ref=dst, send_sem=send, recv_sem=recv,
            device_id={"prow": pp, "pcol": qq}, device_id_type=pl.DeviceIdType.MESH,
        )

    def peer(d):
        return lax.rem(p + d, np_)

    def load(h, r):
        at = pl.ds(r * ROWS, ROWS)
        return pltpu.make_async_copy(
            block.at[at, pl.ds(h * HALF, HALF)], panel.at[h, at], load_sem.at[h * steps + r]
        )

    def load_blk(r):
        at = pl.ds(r * ROWS, ROWS)
        return pltpu.make_async_copy(block.at[at], blk.at[at], blk_sem.at[r])

    def pass_on(h, r):
        at = pl.ds(r * ROWS, ROWS)
        c = h * steps + r
        return remote(panel.at[h, at], panel.at[h, at], csend.at[c], crecv.at[c], p, q + 1)

    def gram_part(d):
        j = peer(d)
        return remote(
            gram.at[pl.ds(pl.multiple_of(j * gs, 8), gs)], gparts.at[p],
            gsend.at[d], grecv.at[p], j, q,
        )

    def gram_wait(d):
        j = peer(d)
        return remote(
            gram.at[pl.ds(0, gs)], gparts.at[j], gsend.at[d], grecv.at[j], j, q
        )

    def spread_rows(ref, size, send, recv, d):
        at = pl.ds(pl.multiple_of(p * size, 8), size)
        return remote(ref.at[at], ref.at[at], send.at[d], recv.at[p], peer(d), q)

    def spread_wait(ref, size, send, recv, d):
        j = peer(d)
        at = pl.ds(pl.multiple_of(j * size, 8), size)
        return remote(ref.at[at], ref.at[at], send.at[d], recv.at[j], j, q)

    def prod_part(h, d):
        j = peer(d)
        return remote(
            acc.at[h, pl.ds(pl.multiple_of(j * ps, 8), ps)], parts.at[h, p],
            psend.at[h, d], precv.at[h, p], j, q,
        )

    def prod_wait(h, d):
        j = peer(d)
        return remote(
            acc.at[h, pl.ds(0, ps)], parts.at[h, j], psend.at[h, d], precv.at[h, j], j, q
        )

    own_l = pl.ds(pl.multiple_of(p * gs, 8), gs)

    def linv_on():
        return remote(linv.at[own_l], linv.at[own_l], zsend, zrecv, p, q + 1)

    @pl.when(first)
    def _():
        for h in range(2):
            for r in range(steps):
                load(h, r).start()

    for r in range(steps):
        load_blk(r).start()

    barrier = pltpu.get_barrier_semaphore()
    for d in range(1, np_):
        pl.semaphore_signal(
            barrier, inc=1, device_id={"prow": peer(d), "pcol": q},
            device_id_type=pl.DeviceIdType.MESH,
        )

    @pl.when(inner)
    def _():
        pl.semaphore_signal(
            barrier, inc=1, device_id={"prow": p, "pcol": q - 1},
            device_id_type=pl.DeviceIdType.MESH,
        )

    @pl.when(sends_on)
    def _():
        pl.semaphore_signal(
            barrier, inc=1, device_id={"prow": p, "pcol": q + 1},
            device_id_type=pl.DeviceIdType.MESH,
        )

    pl.semaphore_wait(
        barrier, np_ - 1 + jnp.where(inner, 1, 0) + jnp.where(sends_on, 1, 0)
    )

    @pl.when(first)
    def _():
        for h in range(2):
            for r in range(steps):
                load(h, r).wait()
                if nq > 1:
                    pass_on(h, r).start()
        gram[...] = jnp.zeros_like(gram)

        @pl.loop(0, steps)
        def _(r):
            at = pl.ds(pl.multiple_of(r * ROWS, ROWS), ROWS)
            both = jnp.concatenate([panel[0, at, :], panel[1, at, :]], axis=1)
            gram[...] += jnp.dot(both.T, both, precision=HIGHEST, preferred_element_type=F32)

        for d in range(1, np_):
            gram_part(d).start()
        total = gram[own_l, :]
        for d in range(1, np_):
            gram_wait(d).wait_recv()
            total = total + gparts[peer(d)]
        gfull[own_l, :] = total
        for d in range(1, np_):
            spread_rows(gfull, gs, hsend, hrecv, d).start()
        for d in range(1, np_):
            spread_wait(gfull, gs, hsend, hrecv, d).wait_recv()
        work[:, :NB] = gfull[...]
        work[:, NB:] = (
            lax.broadcasted_iota(jnp.int32, (NB, NB), 0)
            == lax.broadcasted_iota(jnp.int32, (NB, NB), 1)
        ).astype(F32)
        inverse_cholesky(work)
        linv[...] = work[:, NB:]
        if nq > 1:
            linv_on().start()
        for d in range(1, np_):
            gram_part(d).wait_send()
            spread_rows(gfull, gs, hsend, hrecv, d).wait_send()

    acc[...] = jnp.zeros_like(acc)

    def reduce_start(h):
        for d in range(1, np_):
            prod_part(h, d).start()

    def reduce_end(h):
        own = pl.ds(pl.multiple_of(p * ps, 8), ps)
        total = acc[h, own, :]
        for d in range(1, np_):
            prod_wait(h, d).wait_recv()
            total = total + parts[h, peer(d)]
        prod[h, own, :] = total
        for d in range(1, np_):
            spread_rows(prod.at[h], ps, asend.at[h], arecv.at[h], d).start()

    for h in range(2):

        @pl.loop(0, steps)
        def _(r):
            at = pl.ds(pl.multiple_of(r * ROWS, ROWS), ROWS)

            @pl.when(inner)
            def _():
                pass_on(h, r).wait_recv()

            @pl.when(jnp.logical_and(inner, sends_on))
            def _():
                pass_on(h, r).start()

            if h == 0:
                load_blk(r).wait()
            left = split(panel[h, at, :].T)
            for c in range(0, cols, 256):
                right = split(blk[at, c : c + 256])
                acc[h, :, c : c + 256] += dot3(left, right)

            if h == 1:

                @pl.when(r == steps // 2)
                def _():
                    reduce_end(0)

        reduce_start(h)

    panel_copy = pltpu.make_async_copy(panel, panel_out, out_sem.at[0])
    panel_copy.start()

    @pl.when(inner)
    def _():
        linv_on().wait_recv()

        @pl.when(sends_on)
        def _():
            linv_on().start()

        for d in range(1, np_):
            spread_rows(linv, gs, lsend, lrecv, d).start()

    reduce_end(1)

    @pl.when(inner)
    def _():
        for d in range(1, np_):
            spread_wait(linv, gs, lsend, lrecv, d).wait_recv()

    linv_copy = pltpu.make_async_copy(linv, linv_out, out_sem.at[1])
    linv_copy.start()
    for h in range(2):
        for d in range(1, np_):
            spread_wait(prod.at[h], ps, asend.at[h], arecv.at[h], d).wait_recv()
    prod_copy = pltpu.make_async_copy(prod, prod_out, out_sem.at[2])
    prod_copy.start()

    for h in range(2):
        for d in range(1, np_):
            prod_part(h, d).wait_send()
            spread_rows(prod.at[h], ps, asend.at[h], arecv.at[h], d).wait_send()

    @pl.when(inner)
    def _():
        for d in range(1, np_):
            spread_rows(linv, gs, lsend, lrecv, d).wait_send()

    @pl.when(sends_on)
    def _():
        for h in range(2):
            for r in range(steps):
                pass_on(h, r).wait_send()
        linv_on().wait_send()

    panel_copy.wait()
    linv_copy.wait()
    prod_copy.wait()


def update_kernel(block, panel, linv, prod, top, updated, left_inv, right_top):
    cols = block.shape[1]

    @pl.when(pl.program_id(0) == 0)
    def _():
        for c in range(0, cols, 256):
            at = slice(c, c + 256)
            products = jnp.concatenate([prod[0, :, at], prod[1, :, at]], axis=0)
            tile = jnp.dot(linv[...], products, precision=HIGHEST, preferred_element_type=F32)
            top[:, at] = tile
            right_top[0, :, at], right_top[1, :, at] = split(tile)
        left_inv[0], left_inv[1] = split(linv[...].T)

    both = jnp.concatenate([panel[0], panel[1]], axis=1)
    basis = dot3(split(both), (left_inv[0], left_inv[1]))
    left = split(basis)
    for c in range(0, cols, 256):
        at = slice(c, c + 256)
        right = (right_top[0, :, at], right_top[1, :, at])
        updated[:, at] = block[:, at] - dot3(left, right)

    @pl.when(lax.axis_index("pcol") == 0)
    def _():
        updated[:, :NB] = basis


def body(np_, nq, block):
    rows, cols = block.shape
    steps = rows // ROWS
    gs = NB // np_
    ps = HALF // np_
    dma = pltpu.SemaphoreType.DMA
    hbm = pl.BlockSpec(memory_space=pl.ANY)
    flops = 3 * 2 * rows * NB * cols
    panel, linv, prod = pl.pallas_call(
        functools.partial(gather_kernel, np_, nq),
        out_shape=(
            jax.ShapeDtypeStruct((2, rows, HALF), F32),
            jax.ShapeDtypeStruct((NB, NB), F32),
            jax.ShapeDtypeStruct((2, HALF, cols), F32),
        ),
        in_specs=[hbm],
        out_specs=(hbm, hbm, hbm),
        scratch_shapes=[
            pltpu.VMEM((rows, cols), F32),
            pltpu.VMEM((2, rows, HALF), F32),
            pltpu.VMEM((2, HALF, cols), F32),
            pltpu.VMEM((2, np_, ps, cols), F32),
            pltpu.VMEM((2, HALF, cols), F32),
            pltpu.VMEM((NB, NB), F32),
            pltpu.VMEM((np_, gs, NB), F32),
            pltpu.VMEM((NB, NB), F32),
            pltpu.VMEM((NB, 2 * NB), F32),
            pltpu.VMEM((NB, NB), F32),
            dma((2 * steps,)),
            dma((steps,)),
            dma((2 * steps,)),
            dma((2 * steps,)),
            dma((np_,)),
            dma((np_,)),
            dma((np_,)),
            dma((np_,)),
            dma((2, np_)),
            dma((2, np_)),
            dma((2, np_)),
            dma((2, np_)),
            dma,
            dma,
            dma((np_,)),
            dma((np_,)),
            dma((3,)),
        ],
        compiler_params=pltpu.CompilerParams(
            collective_id=0, has_side_effects=True, vmem_limit_bytes=32 * 2**20
        ),
        cost_estimate=pl.CostEstimate(
            flops=flops, bytes_accessed=4 * rows * cols, transcendentals=0
        ),
    )(block)
    whole = lambda *shape: pl.BlockSpec(shape, lambda i: (0,) * len(shape))
    return pl.pallas_call(
        update_kernel,
        grid=(steps,),
        out_shape=(
            jax.ShapeDtypeStruct((NB, cols), F32),
            jax.ShapeDtypeStruct((rows, cols), F32),
        ),
        in_specs=[
            pl.BlockSpec((ROWS, cols), lambda i: (i, 0)),
            pl.BlockSpec((2, ROWS, HALF), lambda i: (0, i, 0)),
            whole(NB, NB),
            whole(2, HALF, cols),
        ],
        out_specs=(whole(NB, cols), pl.BlockSpec((ROWS, cols), lambda i: (i, 0))),
        scratch_shapes=[
            pltpu.VMEM((2, NB, NB), jnp.bfloat16),
            pltpu.VMEM((2, NB, cols), jnp.bfloat16),
        ],
        compiler_params=pltpu.CompilerParams(vmem_limit_bytes=32 * 2**20),
        cost_estimate=pl.CostEstimate(
            flops=flops, bytes_accessed=8 * rows * cols, transcendentals=0
        ),
    )(block, panel, linv, prod)


def solution(mesh):
    return jax.shard_map(
        functools.partial(body, mesh.shape["prow"], mesh.shape["pcol"]),
        mesh=mesh,
        in_specs=(P("prow", "pcol"),),
        out_specs=(P(None, "pcol"), P("prow", "pcol")),
        check_vma=False,
    )
```

```python
import functools

import jax
import jax.numpy as jnp
from jax import lax
from jax.experimental import pallas as pl
from jax.experimental.pallas import tpu as pltpu
from jax.sharding import PartitionSpec as P

NB = 256
HALF = 128
ROWS = 256
PIECE = 128
DIAG = 64
HIGHEST = lax.Precision.HIGHEST
F32 = jnp.float32


def split(x):
    hi = x.astype(jnp.bfloat16)
    return hi, (x - hi.astype(F32)).astype(jnp.bfloat16)


def left_terms(x):
    hi, lo = split(x)
    return jnp.concatenate([hi, lo, hi], axis=1)


def right_terms(x):
    hi, lo = split(x)
    return jnp.concatenate([hi, hi, lo], axis=0)


def dot3(a, b):
    return jnp.dot(a, b, preferred_element_type=F32)


def inverse_factor(square):
    n = square.shape[0]
    below = lax.broadcasted_iota(jnp.int32, (8, 1), 0)
    eye = (
        lax.broadcasted_iota(jnp.int32, (n, n), 0)
        == lax.broadcasted_iota(jnp.int32, (n, n), 1)
    ).astype(F32)
    rest = jnp.concatenate([square, eye], axis=1)
    done = []
    for g in range(0, n, 8):
        cols = [jnp.broadcast_to(rest[:, k : k + 1], rest.shape) for k in range(g, g + 8)]
        head, rest = rest[:8], rest[8:]
        for j in range(8):
            inv = 1.0 / cols[j][j : j + 1, :]
            row = head[j : j + 1, :] * inv
            if j < 7:
                head = head - jnp.where(below > j, cols[j][:8], 0.0) * row
            if g + 8 < n:
                rest = rest - cols[j][8:] * row
            for i in range(j + 1, 8):
                cols[i] = cols[i] - cols[j] * (cols[i][j : j + 1, :] * inv)
        done.append(head)
    m = jnp.concatenate(done, axis=0)
    pivots = jnp.sum(m[:, :n] * eye, axis=1, keepdims=True)
    return m[:, n:] / jnp.sqrt(pivots)


def inverse_cholesky(work):
    row_id = lax.broadcasted_iota(jnp.int32, (NB, 1), 0)

    @pl.loop(0, NB // DIAG)
    def _(b):
        at = pl.ds(pl.multiple_of(b * DIAG, DIAG), DIAG)
        band = work[at, :]
        square = band[:, :DIAG]
        for other in range(1, NB // DIAG):
            square = jnp.where(b == other, band[:, other * DIAG : (other + 1) * DIAG], square)
        new = jnp.dot(
            inverse_factor(square), band, precision=HIGHEST, preferred_element_type=F32
        )
        lower = jnp.where(row_id >= (b + 1) * DIAG, new[:, :NB].T, 0.0)
        work[...] -= jnp.dot(lower, new, precision=HIGHEST, preferred_element_type=F32)
        work[at, :] = new


def gather_kernel(
    np_, nq, block, panel_out, linv_out, prod_out,
    blk, panel, acc, parts, prod, gram, gparts, gfull, work, linv,
    load_sem, blk_sem, csend, crecv, gsend, grecv, hsend, hrecv,
    psend, precv, asend, arecv, zsend, zrecv, lsend, lrecv, out_sem,
):
    p = lax.axis_index("prow")
    q = lax.axis_index("pcol")
    rows, cols = blk.shape
    steps = rows // ROWS
    pieces = rows // PIECE
    per_step = ROWS // PIECE
    first = q == 0
    inner = q > 0
    sends_on = q < nq - 1
    gs = NB // np_
    ps = HALF // np_

    def remote(src, dst, send, recv, pp, qq):
        return pltpu.make_async_remote_copy(
            src_ref=src, dst_ref=dst, send_sem=send, recv_sem=recv,
            device_id={"prow": pp, "pcol": qq}, device_id_type=pl.DeviceIdType.MESH,
        )

    def peer(d):
        return lax.rem(p + d, np_)

    def load(h, r):
        at = pl.ds(r * PIECE, PIECE)
        return pltpu.make_async_copy(
            block.at[at, pl.ds(h * HALF, HALF)], panel.at[h, at], load_sem.at[h * pieces + r]
        )

    def load_blk(r):
        at = pl.ds(r * ROWS, ROWS)
        return pltpu.make_async_copy(block.at[at], blk.at[at], blk_sem.at[r])

    def pass_on(h, r):
        at = pl.ds(r * PIECE, PIECE)
        c = h * pieces + r
        return remote(panel.at[h, at], panel.at[h, at], csend.at[c], crecv.at[c], p, q + 1)

    def gram_part(d):
        j = peer(d)
        return remote(
            gram.at[pl.ds(pl.multiple_of(j * gs, 8), gs)], gparts.at[p],
            gsend.at[d], grecv.at[p], j, q,
        )

    def gram_wait(d):
        j = peer(d)
        return remote(
            gram.at[pl.ds(0, gs)], gparts.at[j], gsend.at[d], grecv.at[j], j, q
        )

    def spread_rows(ref, size, send, recv, d):
        at = pl.ds(pl.multiple_of(p * size, 8), size)
        return remote(ref.at[at], ref.at[at], send.at[d], recv.at[p], peer(d), q)

    def spread_wait(ref, size, send, recv, d):
        j = peer(d)
        at = pl.ds(pl.multiple_of(j * size, 8), size)
        return remote(ref.at[at], ref.at[at], send.at[d], recv.at[j], j, q)

    def prod_part(h, d):
        j = peer(d)
        return remote(
            acc.at[h, pl.ds(pl.multiple_of(j * ps, 8), ps)], parts.at[h, p],
            psend.at[h, d], precv.at[h, p], j, q,
        )

    def prod_wait(h, d):
        j = peer(d)
        return remote(
            acc.at[h, pl.ds(0, ps)], parts.at[h, j], psend.at[h, d], precv.at[h, j], j, q
        )

    own_l = pl.ds(pl.multiple_of(p * gs, 8), gs)

    def linv_on():
        return remote(linv.at[own_l], linv.at[own_l], zsend, zrecv, p, q + 1)

    @pl.when(first)
    def _():
        for h in range(2):
            for r in range(pieces):
                load(h, r).start()

    for r in range(steps):
        load_blk(r).start()

    barrier = pltpu.get_barrier_semaphore()
    for d in range(1, np_):
        pl.semaphore_signal(
            barrier, inc=1, device_id={"prow": peer(d), "pcol": q},
            device_id_type=pl.DeviceIdType.MESH,
        )

    @pl.when(inner)
    def _():
        pl.semaphore_signal(
            barrier, inc=1, device_id={"prow": p, "pcol": q - 1},
            device_id_type=pl.DeviceIdType.MESH,
        )

    @pl.when(sends_on)
    def _():
        pl.semaphore_signal(
            barrier, inc=1, device_id={"prow": p, "pcol": q + 1},
            device_id_type=pl.DeviceIdType.MESH,
        )

    pl.semaphore_wait(
        barrier, np_ - 1 + jnp.where(inner, 1, 0) + jnp.where(sends_on, 1, 0)
    )

    @pl.when(first)
    def _():
        for h in range(2):
            for r in range(pieces):
                load(h, r).wait()
                if nq > 1:
                    pass_on(h, r).start()
        gram[...] = jnp.zeros_like(gram)

        @pl.loop(0, steps)
        def _(r):
            at = pl.ds(pl.multiple_of(r * ROWS, ROWS), ROWS)
            both = jnp.concatenate([panel[0, at, :], panel[1, at, :]], axis=1)
            gram[...] += jnp.dot(both.T, both, precision=HIGHEST, preferred_element_type=F32)

        for d in range(1, np_):
            gram_part(d).start()
        total = gram[own_l, :]
        for d in range(1, np_):
            gram_wait(d).wait_recv()
            total = total + gparts[peer(d)]
        gfull[own_l, :] = total
        for d in range(1, np_):
            spread_rows(gfull, gs, hsend, hrecv, d).start()
        for d in range(1, np_):
            spread_wait(gfull, gs, hsend, hrecv, d).wait_recv()
        work[:, :NB] = gfull[...]
        work[:, NB:] = (
            lax.broadcasted_iota(jnp.int32, (NB, NB), 0)
            == lax.broadcasted_iota(jnp.int32, (NB, NB), 1)
        ).astype(F32)
        inverse_cholesky(work)
        linv[...] = work[:, NB:]
        if nq > 1:
            linv_on().start()
        for d in range(1, np_):
            gram_part(d).wait_send()
            spread_rows(gfull, gs, hsend, hrecv, d).wait_send()

    acc[...] = jnp.zeros_like(acc)

    def reduce_start(h):
        for d in range(1, np_):
            prod_part(h, d).start()

    def reduce_end(h):
        own = pl.ds(pl.multiple_of(p * ps, 8), ps)
        total = acc[h, own, :]
        for d in range(1, np_):
            prod_wait(h, d).wait_recv()
            total = total + parts[h, peer(d)]
        prod[h, own, :] = total
        for d in range(1, np_):
            spread_rows(prod.at[h], ps, asend.at[h], arecv.at[h], d).start()

    for h in range(2):

        @pl.loop(0, steps)
        def _(r):
            at = pl.ds(pl.multiple_of(r * ROWS, ROWS), ROWS)

            for piece in range(per_step):

                @pl.when(inner)
                def _():
                    pass_on(h, r * per_step + piece).wait_recv()

                @pl.when(jnp.logical_and(inner, sends_on))
                def _():
                    pass_on(h, r * per_step + piece).start()

            if h == 0:
                load_blk(r).wait()
            left = left_terms(panel[h, at, :].T)
            for c in range(0, cols, 256):
                right = right_terms(blk[at, c : c + 256])
                acc[h, :, c : c + 256] += dot3(left, right)

            if h == 1:

                @pl.when(r == steps // 2)
                def _():
                    reduce_end(0)

        reduce_start(h)

    panel_copy = pltpu.make_async_copy(panel, panel_out, out_sem.at[0])
    panel_copy.start()

    @pl.when(inner)
    def _():
        linv_on().wait_recv()

        @pl.when(sends_on)
        def _():
            linv_on().start()

        for d in range(1, np_):
            spread_rows(linv, gs, lsend, lrecv, d).start()

    reduce_end(1)

    @pl.when(inner)
    def _():
        for d in range(1, np_):
            spread_wait(linv, gs, lsend, lrecv, d).wait_recv()

    linv_copy = pltpu.make_async_copy(linv, linv_out, out_sem.at[1])
    linv_copy.start()
    for h in range(2):
        for d in range(1, np_):
            spread_wait(prod.at[h], ps, asend.at[h], arecv.at[h], d).wait_recv()
    prod_copy = pltpu.make_async_copy(prod, prod_out, out_sem.at[2])
    prod_copy.start()

    for h in range(2):
        for d in range(1, np_):
            prod_part(h, d).wait_send()
            spread_rows(prod.at[h], ps, asend.at[h], arecv.at[h], d).wait_send()

    @pl.when(inner)
    def _():
        for d in range(1, np_):
            spread_rows(linv, gs, lsend, lrecv, d).wait_send()

    @pl.when(sends_on)
    def _():
        for h in range(2):
            for r in range(pieces):
                pass_on(h, r).wait_send()
        linv_on().wait_send()

    panel_copy.wait()
    linv_copy.wait()
    prod_copy.wait()


def update_kernel(block, panel, linv, prod, top, updated, right_inv, right_top):
    cols = block.shape[1]

    @pl.when(pl.program_id(0) == 0)
    def _():
        for c in range(0, cols, 256):
            at = slice(c, c + 256)
            products = jnp.concatenate([prod[0, :, at], prod[1, :, at]], axis=0)
            tile = jnp.dot(linv[...], products, precision=HIGHEST, preferred_element_type=F32)
            top[:, at] = tile
            right_top[:, at] = right_terms(tile)
        right_inv[...] = right_terms(linv[...].T)

    both = jnp.concatenate([panel[0], panel[1]], axis=1)
    basis = dot3(left_terms(both), right_inv[...])
    left = left_terms(basis)
    for c in range(0, cols, 256):
        at = slice(c, c + 256)
        updated[:, at] = block[:, at] - dot3(left, right_top[:, at])

    @pl.when(lax.axis_index("pcol") == 0)
    def _():
        updated[:, :NB] = basis


def body(np_, nq, block):
    rows, cols = block.shape
    steps = rows // ROWS
    pieces = rows // PIECE
    gs = NB // np_
    ps = HALF // np_
    dma = pltpu.SemaphoreType.DMA
    hbm = pl.BlockSpec(memory_space=pl.ANY)
    flops = 3 * 2 * rows * NB * cols
    panel, linv, prod = pl.pallas_call(
        functools.partial(gather_kernel, np_, nq),
        out_shape=(
            jax.ShapeDtypeStruct((2, rows, HALF), F32),
            jax.ShapeDtypeStruct((NB, NB), F32),
            jax.ShapeDtypeStruct((2, HALF, cols), F32),
        ),
        in_specs=[hbm],
        out_specs=(hbm, hbm, hbm),
        scratch_shapes=[
            pltpu.VMEM((rows, cols), F32),
            pltpu.VMEM((2, rows, HALF), F32),
            pltpu.VMEM((2, HALF, cols), F32),
            pltpu.VMEM((2, np_, ps, cols), F32),
            pltpu.VMEM((2, HALF, cols), F32),
            pltpu.VMEM((NB, NB), F32),
            pltpu.VMEM((np_, gs, NB), F32),
            pltpu.VMEM((NB, NB), F32),
            pltpu.VMEM((NB, 2 * NB), F32),
            pltpu.VMEM((NB, NB), F32),
            dma((2 * pieces,)),
            dma((steps,)),
            dma((2 * pieces,)),
            dma((2 * pieces,)),
            dma((np_,)),
            dma((np_,)),
            dma((np_,)),
            dma((np_,)),
            dma((2, np_)),
            dma((2, np_)),
            dma((2, np_)),
            dma((2, np_)),
            dma,
            dma,
            dma((np_,)),
            dma((np_,)),
            dma((3,)),
        ],
        compiler_params=pltpu.CompilerParams(
            collective_id=0, has_side_effects=True, vmem_limit_bytes=60 * 2**20
        ),
        cost_estimate=pl.CostEstimate(
            flops=flops, bytes_accessed=4 * rows * cols, transcendentals=0
        ),
    )(block)
    whole = lambda *shape: pl.BlockSpec(shape, lambda i: (0,) * len(shape))
    return pl.pallas_call(
        update_kernel,
        grid=(steps,),
        out_shape=(
            jax.ShapeDtypeStruct((NB, cols), F32),
            jax.ShapeDtypeStruct((rows, cols), F32),
        ),
        in_specs=[
            pl.BlockSpec((ROWS, cols), lambda i: (i, 0)),
            pl.BlockSpec((2, ROWS, HALF), lambda i: (0, i, 0)),
            whole(NB, NB),
            whole(2, HALF, cols),
        ],
        out_specs=(whole(NB, cols), pl.BlockSpec((ROWS, cols), lambda i: (i, 0))),
        scratch_shapes=[
            pltpu.VMEM((3 * NB, NB), jnp.bfloat16),
            pltpu.VMEM((3 * NB, cols), jnp.bfloat16),
        ],
        compiler_params=pltpu.CompilerParams(vmem_limit_bytes=60 * 2**20),
        cost_estimate=pl.CostEstimate(
            flops=flops, bytes_accessed=8 * rows * cols, transcendentals=0
        ),
    )(block, panel, linv, prod)


def solution(mesh):
    return jax.shard_map(
        functools.partial(body, mesh.shape["prow"], mesh.shape["pcol"]),
        mesh=mesh,
        in_specs=(P("prow", "pcol"),),
        out_specs=(P(None, "pcol"), P("prow", "pcol")),
        check_vma=False,
    )
```

```python
import functools

import jax
import jax.numpy as jnp
from jax import lax
from jax.experimental import pallas as pl
from jax.experimental.pallas import tpu as pltpu
from jax.sharding import PartitionSpec as P

NB = 256
HALF = 128
ROWS = 256
PIECE = 128
DIAG = 64
HIGHEST = lax.Precision.HIGHEST
F32 = jnp.float32


def split(x):
    hi = x.astype(jnp.bfloat16)
    return hi, (x - hi.astype(F32)).astype(jnp.bfloat16)


def left_terms(x):
    hi, lo = split(x)
    return jnp.concatenate([hi, lo, hi], axis=1)


def right_terms(x):
    hi, lo = split(x)
    return jnp.concatenate([hi, hi, lo], axis=0)


def dot3(a, b):
    return jnp.dot(a, b, preferred_element_type=F32)


def inverse_factor(square):
    n = square.shape[0]
    below = lax.broadcasted_iota(jnp.int32, (8, 1), 0)
    eye = (
        lax.broadcasted_iota(jnp.int32, (n, n), 0)
        == lax.broadcasted_iota(jnp.int32, (n, n), 1)
    ).astype(F32)
    rest = jnp.concatenate([square, eye], axis=1)
    done = []
    for g in range(0, n, 8):
        cols = [jnp.broadcast_to(rest[:, k : k + 1], rest.shape) for k in range(g, g + 8)]
        head, rest = rest[:8], rest[8:]
        for j in range(8):
            inv = 1.0 / cols[j][j : j + 1, :]
            row = head[j : j + 1, :] * inv
            if j < 7:
                head = head - jnp.where(below > j, cols[j][:8], 0.0) * row
            if g + 8 < n:
                rest = rest - cols[j][8:] * row
            for i in range(j + 1, 8):
                cols[i] = cols[i] - cols[j] * (cols[i][j : j + 1, :] * inv)
        done.append(head)
    m = jnp.concatenate(done, axis=0)
    pivots = jnp.sum(m[:, :n] * eye, axis=1, keepdims=True)
    return m[:, n:] / jnp.sqrt(pivots)


def inverse_cholesky(work):
    row_id = lax.broadcasted_iota(jnp.int32, (NB, 1), 0)

    @pl.loop(0, NB // DIAG)
    def _(b):
        at = pl.ds(pl.multiple_of(b * DIAG, DIAG), DIAG)
        band = work[at, :]
        square = band[:, :DIAG]
        for other in range(1, NB // DIAG):
            square = jnp.where(b == other, band[:, other * DIAG : (other + 1) * DIAG], square)
        new = jnp.dot(
            inverse_factor(square), band, precision=HIGHEST, preferred_element_type=F32
        )
        lower = jnp.where(row_id >= (b + 1) * DIAG, new[:, :NB].T, 0.0)
        work[...] -= jnp.dot(lower, new, precision=HIGHEST, preferred_element_type=F32)
        work[at, :] = new


def gather_kernel(
    np_, nq, block, panel_out, linv_out, prod_out,
    blk, panel, acc, parts, prod, gram, gparts, gfull, work, linv,
    load_sem, blk_sem, csend, crecv, gsend, grecv, hsend, hrecv,
    psend, precv, asend, arecv, zsend, zrecv, lsend, lrecv, out_sem,
):
    p = lax.axis_index("prow")
    q = lax.axis_index("pcol")
    rows, cols = blk.shape
    steps = rows // ROWS
    pieces = rows // PIECE
    per_step = ROWS // PIECE
    ahead = pieces + pieces // 2
    first = q == 0
    inner = q > 0
    sends_on = q < nq - 1
    gs = NB // np_
    ps = HALF // np_

    def remote(src, dst, send, recv, pp, qq):
        return pltpu.make_async_remote_copy(
            src_ref=src, dst_ref=dst, send_sem=send, recv_sem=recv,
            device_id={"prow": pp, "pcol": qq}, device_id_type=pl.DeviceIdType.MESH,
        )

    def peer(d):
        return lax.rem(p + d, np_)

    def load(h, r):
        at = pl.ds(r * PIECE, PIECE)
        return pltpu.make_async_copy(
            block.at[at, pl.ds(h * HALF, HALF)], panel.at[h, at], load_sem.at[h * pieces + r]
        )

    def load_blk(r):
        at = pl.ds(r * ROWS, ROWS)
        return pltpu.make_async_copy(block.at[at], blk.at[at], blk_sem.at[r])

    def pass_on(h, r):
        at = pl.ds(r * PIECE, PIECE)
        c = h * pieces + r
        return remote(panel.at[h, at], panel.at[h, at], csend.at[c], crecv.at[c], p, q + 1)

    def gram_part(d):
        j = peer(d)
        return remote(
            gram.at[pl.ds(pl.multiple_of(j * gs, 8), gs)], gparts.at[p],
            gsend.at[d], grecv.at[p], j, q,
        )

    def gram_wait(d):
        j = peer(d)
        return remote(
            gram.at[pl.ds(0, gs)], gparts.at[j], gsend.at[d], grecv.at[j], j, q
        )

    def spread_rows(ref, size, send, recv, d):
        at = pl.ds(pl.multiple_of(p * size, 8), size)
        return remote(ref.at[at], ref.at[at], send.at[d], recv.at[p], peer(d), q)

    def spread_wait(ref, size, send, recv, d):
        j = peer(d)
        at = pl.ds(pl.multiple_of(j * size, 8), size)
        return remote(ref.at[at], ref.at[at], send.at[d], recv.at[j], j, q)

    def prod_part(h, d):
        j = peer(d)
        return remote(
            acc.at[h, pl.ds(pl.multiple_of(j * ps, 8), ps)], parts.at[h, p],
            psend.at[h, d], precv.at[h, p], j, q,
        )

    def prod_wait(h, d):
        j = peer(d)
        return remote(
            acc.at[h, pl.ds(0, ps)], parts.at[h, j], psend.at[h, d], precv.at[h, j], j, q
        )

    own_l = pl.ds(pl.multiple_of(p * gs, 8), gs)

    def linv_on():
        return remote(linv.at[own_l], linv.at[own_l], zsend, zrecv, p, q + 1)

    @pl.when(first)
    def _():
        for h in range(2):
            for r in range(pieces):
                load(h, r).start()

    for r in range(steps):
        load_blk(r).start()

    barrier = pltpu.get_barrier_semaphore()
    for d in range(1, np_):
        pl.semaphore_signal(
            barrier, inc=1, device_id={"prow": peer(d), "pcol": q},
            device_id_type=pl.DeviceIdType.MESH,
        )

    @pl.when(inner)
    def _():
        pl.semaphore_signal(
            barrier, inc=1, device_id={"prow": p, "pcol": q - 1},
            device_id_type=pl.DeviceIdType.MESH,
        )

    @pl.when(sends_on)
    def _():
        pl.semaphore_signal(
            barrier, inc=1, device_id={"prow": p, "pcol": q + 1},
            device_id_type=pl.DeviceIdType.MESH,
        )

    pl.semaphore_wait(
        barrier, np_ - 1 + jnp.where(inner, 1, 0) + jnp.where(sends_on, 1, 0)
    )

    @pl.when(first)
    def _():
        for h in range(2):
            for r in range(pieces):
                load(h, r).wait()
                if nq > 1 and h * pieces + r < ahead:
                    pass_on(h, r).start()
        gram[...] = jnp.zeros_like(gram)

        @pl.loop(0, steps)
        def _(r):
            at = pl.ds(pl.multiple_of(r * ROWS, ROWS), ROWS)
            both = jnp.concatenate([panel[0, at, :], panel[1, at, :]], axis=1)
            gram[...] += jnp.dot(both.T, both, precision=HIGHEST, preferred_element_type=F32)

        for d in range(1, np_):
            gram_part(d).start()
        total = gram[own_l, :]
        for d in range(1, np_):
            gram_wait(d).wait_recv()
            total = total + gparts[peer(d)]
        gfull[own_l, :] = total
        for d in range(1, np_):
            spread_rows(gfull, gs, hsend, hrecv, d).start()
        for d in range(1, np_):
            spread_wait(gfull, gs, hsend, hrecv, d).wait_recv()
        work[:, :NB] = gfull[...]
        work[:, NB:] = (
            lax.broadcasted_iota(jnp.int32, (NB, NB), 0)
            == lax.broadcasted_iota(jnp.int32, (NB, NB), 1)
        ).astype(F32)
        inverse_cholesky(work)
        linv[...] = work[:, NB:]
        if nq > 1:
            linv_on().start()
            for r in range(ahead - pieces, pieces):
                pass_on(1, r).start()
        for d in range(1, np_):
            gram_part(d).wait_send()
            spread_rows(gfull, gs, hsend, hrecv, d).wait_send()

    acc[...] = jnp.zeros_like(acc)

    def reduce_start(h):
        for d in range(1, np_):
            prod_part(h, d).start()

    def reduce_end(h):
        own = pl.ds(pl.multiple_of(p * ps, 8), ps)
        total = acc[h, own, :]
        for d in range(1, np_):
            prod_wait(h, d).wait_recv()
            total = total + parts[h, peer(d)]
        prod[h, own, :] = total
        for d in range(1, np_):
            spread_rows(prod.at[h], ps, asend.at[h], arecv.at[h], d).start()

    def linv_forward():
        @pl.when(inner)
        def _():
            linv_on().wait_recv()

            @pl.when(sends_on)
            def _():
                linv_on().start()

            for d in range(1, np_):
                spread_rows(linv, gs, lsend, lrecv, d).start()

    for h in range(2):

        @pl.loop(0, steps)
        def _(r):
            at = pl.ds(pl.multiple_of(r * ROWS, ROWS), ROWS)

            for piece in range(per_step):

                @pl.when(inner)
                def _():
                    pass_on(h, r * per_step + piece).wait_recv()

                @pl.when(jnp.logical_and(inner, sends_on))
                def _():
                    pass_on(h, r * per_step + piece).start()

            if h == 0:
                load_blk(r).wait()
            left = left_terms(panel[h, at, :].T)
            for c in range(0, cols, 256):
                right = right_terms(blk[at, c : c + 256])
                acc[h, :, c : c + 256] += dot3(left, right)

            if h == 1:

                @pl.when(r == steps // 2)
                def _():
                    reduce_end(0)
                    linv_forward()

        reduce_start(h)

    panel_copy = pltpu.make_async_copy(panel, panel_out, out_sem.at[0])
    panel_copy.start()

    reduce_end(1)

    @pl.when(inner)
    def _():
        for d in range(1, np_):
            spread_wait(linv, gs, lsend, lrecv, d).wait_recv()

    linv_copy = pltpu.make_async_copy(linv, linv_out, out_sem.at[1])
    linv_copy.start()
    for h in range(2):
        for d in range(1, np_):
            spread_wait(prod.at[h], ps, asend.at[h], arecv.at[h], d).wait_recv()
    prod_copy = pltpu.make_async_copy(prod, prod_out, out_sem.at[2])
    prod_copy.start()

    for h in range(2):
        for d in range(1, np_):
            prod_part(h, d).wait_send()
            spread_rows(prod.at[h], ps, asend.at[h], arecv.at[h], d).wait_send()

    @pl.when(inner)
    def _():
        for d in range(1, np_):
            spread_rows(linv, gs, lsend, lrecv, d).wait_send()

    @pl.when(sends_on)
    def _():
        for h in range(2):
            for r in range(pieces):
                pass_on(h, r).wait_send()
        linv_on().wait_send()

    panel_copy.wait()
    linv_copy.wait()
    prod_copy.wait()


def update_kernel(block, panel, linv, prod, top, updated, basis, left, right_top):
    i, c = pl.program_id(0), pl.program_id(1)

    @pl.when(c == 0)
    def _():
        both = jnp.concatenate([panel[0], panel[1]], axis=1)
        basis[...] = dot3(left_terms(both), right_terms(linv[...].T))
        left[...] = left_terms(basis[...])

    @pl.when(i == 0)
    def _():
        products = jnp.concatenate([prod[0], prod[1]], axis=0)
        tile = jnp.dot(linv[...], products, precision=HIGHEST, preferred_element_type=F32)
        top[...] = tile
        right_top[c] = right_terms(tile)

    in_panel = jnp.logical_and(c == 0, lax.axis_index("pcol") == 0)

    @pl.when(in_panel)
    def _():
        updated[...] = basis[...]

    @pl.when(jnp.logical_not(in_panel))
    def _():
        updated[...] = block[...] - dot3(left[...], right_top[c])


def body(np_, nq, block):
    rows, cols = block.shape
    steps = rows // ROWS
    pieces = rows // PIECE
    gs = NB // np_
    ps = HALF // np_
    dma = pltpu.SemaphoreType.DMA
    hbm = pl.BlockSpec(memory_space=pl.ANY)
    flops = 3 * 2 * rows * NB * cols
    panel, linv, prod = pl.pallas_call(
        functools.partial(gather_kernel, np_, nq),
        out_shape=(
            jax.ShapeDtypeStruct((2, rows, HALF), F32),
            jax.ShapeDtypeStruct((NB, NB), F32),
            jax.ShapeDtypeStruct((2, HALF, cols), F32),
        ),
        in_specs=[hbm],
        out_specs=(hbm, hbm, hbm),
        scratch_shapes=[
            pltpu.VMEM((rows, cols), F32),
            pltpu.VMEM((2, rows, HALF), F32),
            pltpu.VMEM((2, HALF, cols), F32),
            pltpu.VMEM((2, np_, ps, cols), F32),
            pltpu.VMEM((2, HALF, cols), F32),
            pltpu.VMEM((NB, NB), F32),
            pltpu.VMEM((np_, gs, NB), F32),
            pltpu.VMEM((NB, NB), F32),
            pltpu.VMEM((NB, 2 * NB), F32),
            pltpu.VMEM((NB, NB), F32),
            dma((2 * pieces,)),
            dma((steps,)),
            dma((2 * pieces,)),
            dma((2 * pieces,)),
            dma((np_,)),
            dma((np_,)),
            dma((np_,)),
            dma((np_,)),
            dma((2, np_)),
            dma((2, np_)),
            dma((2, np_)),
            dma((2, np_)),
            dma,
            dma,
            dma((np_,)),
            dma((np_,)),
            dma((3,)),
        ],
        compiler_params=pltpu.CompilerParams(
            collective_id=0, has_side_effects=True, vmem_limit_bytes=60 * 2**20
        ),
        cost_estimate=pl.CostEstimate(
            flops=flops, bytes_accessed=4 * rows * cols, transcendentals=0
        ),
    )(block)
    tall, tiles = rows // 2, cols // NB
    return pl.pallas_call(
        update_kernel,
        grid=(rows // tall, tiles),
        out_shape=(
            jax.ShapeDtypeStruct((NB, cols), F32),
            jax.ShapeDtypeStruct((rows, cols), F32),
        ),
        in_specs=[
            pl.BlockSpec((tall, NB), lambda i, c: (i, c)),
            pl.BlockSpec((2, tall, HALF), lambda i, c: (0, i, 0)),
            pl.BlockSpec((NB, NB), lambda i, c: (0, 0)),
            pl.BlockSpec((2, HALF, NB), lambda i, c: (0, 0, jnp.where(i == 0, c, tiles - 1))),
        ],
        out_specs=(
            pl.BlockSpec((NB, NB), lambda i, c: (0, jnp.where(i == 0, c, tiles - 1))),
            pl.BlockSpec((tall, NB), lambda i, c: (i, c)),
        ),
        scratch_shapes=[
            pltpu.VMEM((tall, NB), F32),
            pltpu.VMEM((tall, 3 * NB), jnp.bfloat16),
            pltpu.VMEM((tiles, 3 * NB, NB), jnp.bfloat16),
        ],
        compiler_params=pltpu.CompilerParams(vmem_limit_bytes=60 * 2**20),
        cost_estimate=pl.CostEstimate(
            flops=flops, bytes_accessed=8 * rows * cols, transcendentals=0
        ),
    )(block, panel, linv, prod)


def solution(mesh):
    return jax.shard_map(
        functools.partial(body, mesh.shape["prow"], mesh.shape["pcol"]),
        mesh=mesh,
        in_specs=(P("prow", "pcol"),),
        out_specs=(P(None, "pcol"), P("prow", "pcol")),
        check_vma=False,
    )
```

```python
import functools

import jax
import jax.numpy as jnp
from jax import lax
from jax.experimental import pallas as pl
from jax.experimental.pallas import tpu as pltpu
from jax.sharding import PartitionSpec as P

NB = 256
HALF = 128
ROWS = 256
PIECE = 128
DIAG = 64
HIGHEST = lax.Precision.HIGHEST
F32 = jnp.float32


def split(x):
    hi = x.astype(jnp.bfloat16)
    return hi, (x - hi.astype(F32)).astype(jnp.bfloat16)


def left_terms(x):
    hi, lo = split(x)
    return jnp.concatenate([hi, lo, hi], axis=1)


def right_terms(x):
    hi, lo = split(x)
    return jnp.concatenate([hi, hi, lo], axis=0)


def dot3(a, b):
    return jnp.dot(a, b, preferred_element_type=F32)


def inverse_factor(square):
    n = square.shape[0]
    below = lax.broadcasted_iota(jnp.int32, (8, 1), 0)
    eye = (
        lax.broadcasted_iota(jnp.int32, (n, n), 0)
        == lax.broadcasted_iota(jnp.int32, (n, n), 1)
    ).astype(F32)
    rest = jnp.concatenate([square, eye], axis=1)
    done = []
    for g in range(0, n, 8):
        cols = [jnp.broadcast_to(rest[:, k : k + 1], rest.shape) for k in range(g, g + 8)]
        head, rest = rest[:8], rest[8:]
        for j in range(8):
            inv = 1.0 / cols[j][j : j + 1, :]
            row = head[j : j + 1, :] * inv
            if j < 7:
                head = head - jnp.where(below > j, cols[j][:8], 0.0) * row
            if g + 8 < n:
                rest = rest - cols[j][8:] * row
            for i in range(j + 1, 8):
                cols[i] = cols[i] - cols[j] * (cols[i][j : j + 1, :] * inv)
        done.append(head)
    m = jnp.concatenate(done, axis=0)
    pivots = jnp.sum(m[:, :n] * eye, axis=1, keepdims=True)
    return m[:, n:] / jnp.sqrt(pivots)


def inverse_cholesky(work):
    row_id = lax.broadcasted_iota(jnp.int32, (NB, 1), 0)

    @pl.loop(0, NB // DIAG)
    def _(b):
        at = pl.ds(pl.multiple_of(b * DIAG, DIAG), DIAG)
        band = work[at, :]
        square = band[:, :DIAG]
        for other in range(1, NB // DIAG):
            square = jnp.where(b == other, band[:, other * DIAG : (other + 1) * DIAG], square)
        new = jnp.dot(
            inverse_factor(square), band, precision=HIGHEST, preferred_element_type=F32
        )
        lower = jnp.where(row_id >= (b + 1) * DIAG, new[:, :NB].T, 0.0)
        work[...] -= jnp.dot(lower, new, precision=HIGHEST, preferred_element_type=F32)
        work[at, :] = new


def gather_kernel(
    np_, nq, block, blk, panel_out, linv_out, prod_out,
    panel, acc, parts, prod, gram, gparts, gfull, work, linv,
    load_sem, blk_sem, csend, crecv, gsend, grecv, hsend, hrecv,
    psend, precv, asend, arecv, zsend, zrecv, lsend, lrecv, out_sem,
):
    p = lax.axis_index("prow")
    q = lax.axis_index("pcol")
    rows, cols = blk.shape
    steps = rows // ROWS
    pieces = rows // PIECE
    per_step = ROWS // PIECE
    ahead = pieces + pieces // 2
    first = q == 0
    inner = q > 0
    sends_on = q < nq - 1
    gs = NB // np_
    ps = HALF // np_

    def remote(src, dst, send, recv, pp, qq):
        return pltpu.make_async_remote_copy(
            src_ref=src, dst_ref=dst, send_sem=send, recv_sem=recv,
            device_id={"prow": pp, "pcol": qq}, device_id_type=pl.DeviceIdType.MESH,
        )

    def peer(d):
        return lax.rem(p + d, np_)

    def load(h, r):
        at = pl.ds(r * PIECE, PIECE)
        return pltpu.make_async_copy(
            block.at[at, pl.ds(h * HALF, HALF)], panel.at[h, at], load_sem.at[h * pieces + r]
        )

    def load_blk(r):
        at = pl.ds(r * ROWS, ROWS)
        return pltpu.make_async_copy(block.at[at], blk.at[at], blk_sem.at[r])

    def pass_on(h, r):
        at = pl.ds(r * PIECE, PIECE)
        c = h * pieces + r
        return remote(panel.at[h, at], panel.at[h, at], csend.at[c], crecv.at[c], p, q + 1)

    def gram_part(d):
        j = peer(d)
        return remote(
            gram.at[pl.ds(pl.multiple_of(j * gs, 8), gs)], gparts.at[p],
            gsend.at[d], grecv.at[p], j, q,
        )

    def gram_wait(d):
        j = peer(d)
        return remote(
            gram.at[pl.ds(0, gs)], gparts.at[j], gsend.at[d], grecv.at[j], j, q
        )

    def spread_rows(ref, size, send, recv, d):
        at = pl.ds(pl.multiple_of(p * size, 8), size)
        return remote(ref.at[at], ref.at[at], send.at[d], recv.at[p], peer(d), q)

    def spread_wait(ref, size, send, recv, d):
        j = peer(d)
        at = pl.ds(pl.multiple_of(j * size, 8), size)
        return remote(ref.at[at], ref.at[at], send.at[d], recv.at[j], j, q)

    def prod_part(h, d):
        j = peer(d)
        return remote(
            acc.at[h, pl.ds(pl.multiple_of(j * ps, 8), ps)], parts.at[h, p],
            psend.at[h, d], precv.at[h, p], j, q,
        )

    def prod_wait(h, d):
        j = peer(d)
        return remote(
            acc.at[h, pl.ds(0, ps)], parts.at[h, j], psend.at[h, d], precv.at[h, j], j, q
        )

    own_l = pl.ds(pl.multiple_of(p * gs, 8), gs)

    def linv_on():
        return remote(linv.at[own_l], linv.at[own_l], zsend, zrecv, p, q + 1)

    @pl.when(first)
    def _():
        for h in range(2):
            for r in range(pieces):
                load(h, r).start()

    for r in range(steps):
        load_blk(r).start()

    barrier = pltpu.get_barrier_semaphore()
    for d in range(1, np_):
        pl.semaphore_signal(
            barrier, inc=1, device_id={"prow": peer(d), "pcol": q},
            device_id_type=pl.DeviceIdType.MESH,
        )

    @pl.when(inner)
    def _():
        pl.semaphore_signal(
            barrier, inc=1, device_id={"prow": p, "pcol": q - 1},
            device_id_type=pl.DeviceIdType.MESH,
        )

    @pl.when(sends_on)
    def _():
        pl.semaphore_signal(
            barrier, inc=1, device_id={"prow": p, "pcol": q + 1},
            device_id_type=pl.DeviceIdType.MESH,
        )

    pl.semaphore_wait(
        barrier, np_ - 1 + jnp.where(inner, 1, 0) + jnp.where(sends_on, 1, 0)
    )

    @pl.when(first)
    def _():
        for h in range(2):
            for r in range(pieces):
                load(h, r).wait()
                if nq > 1 and h * pieces + r < ahead:
                    pass_on(h, r).start()
        gram[...] = jnp.zeros_like(gram)

        @pl.loop(0, steps)
        def _(r):
            at = pl.ds(pl.multiple_of(r * ROWS, ROWS), ROWS)
            both = jnp.concatenate([panel[0, at, :], panel[1, at, :]], axis=1)
            gram[...] += jnp.dot(both.T, both, precision=HIGHEST, preferred_element_type=F32)

        for d in range(1, np_):
            gram_part(d).start()
        total = gram[own_l, :]
        for d in range(1, np_):
            gram_wait(d).wait_recv()
            total = total + gparts[peer(d)]
        gfull[own_l, :] = total
        for d in range(1, np_):
            spread_rows(gfull, gs, hsend, hrecv, d).start()
        for d in range(1, np_):
            spread_wait(gfull, gs, hsend, hrecv, d).wait_recv()
        work[:, :NB] = gfull[...]
        work[:, NB:] = (
            lax.broadcasted_iota(jnp.int32, (NB, NB), 0)
            == lax.broadcasted_iota(jnp.int32, (NB, NB), 1)
        ).astype(F32)
        inverse_cholesky(work)
        linv[...] = work[:, NB:]
        if nq > 1:
            linv_on().start()
            for r in range(ahead - pieces, pieces):
                pass_on(1, r).start()
        for d in range(1, np_):
            gram_part(d).wait_send()
            spread_rows(gfull, gs, hsend, hrecv, d).wait_send()

    acc[...] = jnp.zeros_like(acc)

    def reduce_start(h):
        for d in range(1, np_):
            prod_part(h, d).start()

    def reduce_end(h):
        own = pl.ds(pl.multiple_of(p * ps, 8), ps)
        total = acc[h, own, :]
        for d in range(1, np_):
            prod_wait(h, d).wait_recv()
            total = total + parts[h, peer(d)]
        prod[h, own, :] = total
        for d in range(1, np_):
            spread_rows(prod.at[h], ps, asend.at[h], arecv.at[h], d).start()

    def linv_forward():
        @pl.when(inner)
        def _():
            linv_on().wait_recv()

            @pl.when(sends_on)
            def _():
                linv_on().start()

            for d in range(1, np_):
                spread_rows(linv, gs, lsend, lrecv, d).start()

    for h in range(2):

        @pl.loop(0, steps)
        def _(r):
            at = pl.ds(pl.multiple_of(r * ROWS, ROWS), ROWS)

            for piece in range(per_step):

                @pl.when(inner)
                def _():
                    pass_on(h, r * per_step + piece).wait_recv()

                @pl.when(jnp.logical_and(inner, sends_on))
                def _():
                    pass_on(h, r * per_step + piece).start()

            if h == 0:
                load_blk(r).wait()
            left = left_terms(panel[h, at, :].T)
            for c in range(0, cols, 256):
                right = right_terms(blk[at, c : c + 256])
                acc[h, :, c : c + 256] += dot3(left, right)

            if h == 1:

                @pl.when(r == steps // 2)
                def _():
                    reduce_end(0)
                    linv_forward()

        reduce_start(h)

    panel_copy = pltpu.make_async_copy(panel, panel_out, out_sem.at[0])
    panel_copy.start()

    reduce_end(1)

    @pl.when(inner)
    def _():
        for d in range(1, np_):
            spread_wait(linv, gs, lsend, lrecv, d).wait_recv()

    linv_copy = pltpu.make_async_copy(linv, linv_out, out_sem.at[1])
    linv_copy.start()
    for h in range(2):
        for d in range(1, np_):
            spread_wait(prod.at[h], ps, asend.at[h], arecv.at[h], d).wait_recv()
    prod_copy = pltpu.make_async_copy(prod, prod_out, out_sem.at[2])
    prod_copy.start()

    for h in range(2):
        for d in range(1, np_):
            prod_part(h, d).wait_send()
            spread_rows(prod.at[h], ps, asend.at[h], arecv.at[h], d).wait_send()

    @pl.when(inner)
    def _():
        for d in range(1, np_):
            spread_rows(linv, gs, lsend, lrecv, d).wait_send()

    @pl.when(sends_on)
    def _():
        for h in range(2):
            for r in range(pieces):
                pass_on(h, r).wait_send()
        linv_on().wait_send()

    panel_copy.wait()
    linv_copy.wait()
    prod_copy.wait()


def update_kernel(block, panel, linv, prod, top, updated, basis, left, right_top):
    i, c = pl.program_id(0), pl.program_id(1)
    tall = updated.shape[0]
    down = pl.ds(pl.multiple_of(i * tall, tall), tall)
    across = pl.ds(pl.multiple_of(c * NB, NB), NB)

    @pl.when(c == 0)
    def _():
        both = jnp.concatenate([panel[0, down, :], panel[1, down, :]], axis=1)
        basis[...] = dot3(left_terms(both), right_terms(linv[...].T))
        left[...] = left_terms(basis[...])

    @pl.when(i == 0)
    def _():
        products = jnp.concatenate([prod[0, :, across], prod[1, :, across]], axis=0)
        tile = jnp.dot(linv[...], products, precision=HIGHEST, preferred_element_type=F32)
        top[...] = tile
        right_top[c] = right_terms(tile)

    in_panel = jnp.logical_and(c == 0, lax.axis_index("pcol") == 0)

    @pl.when(in_panel)
    def _():
        updated[...] = basis[...]

    @pl.when(jnp.logical_not(in_panel))
    def _():
        updated[...] = block[down, across] - dot3(left[...], right_top[c])


def body(np_, nq, block):
    rows, cols = block.shape
    steps = rows // ROWS
    pieces = rows // PIECE
    gs = NB // np_
    ps = HALF // np_
    dma = pltpu.SemaphoreType.DMA
    vmem = pl.BlockSpec(memory_space=pltpu.VMEM)
    flops = 3 * 2 * rows * NB * cols
    block, panel, linv, prod = pl.pallas_call(
        functools.partial(gather_kernel, np_, nq),
        out_shape=(
            pltpu.VMEM((rows, cols), F32),
            pltpu.VMEM((2, rows, HALF), F32),
            pltpu.VMEM((NB, NB), F32),
            pltpu.VMEM((2, HALF, cols), F32),
        ),
        in_specs=[pl.BlockSpec(memory_space=pltpu.HBM)],
        out_specs=(vmem,) * 4,
        scratch_shapes=[
            pltpu.VMEM((2, rows, HALF), F32),
            pltpu.VMEM((2, HALF, cols), F32),
            pltpu.VMEM((2, np_, ps, cols), F32),
            pltpu.VMEM((2, HALF, cols), F32),
            pltpu.VMEM((NB, NB), F32),
            pltpu.VMEM((np_, gs, NB), F32),
            pltpu.VMEM((NB, NB), F32),
            pltpu.VMEM((NB, 2 * NB), F32),
            pltpu.VMEM((NB, NB), F32),
            dma((2 * pieces,)),
            dma((steps,)),
            dma((2 * pieces,)),
            dma((2 * pieces,)),
            dma((np_,)),
            dma((np_,)),
            dma((np_,)),
            dma((np_,)),
            dma((2, np_)),
            dma((2, np_)),
            dma((2, np_)),
            dma((2, np_)),
            dma,
            dma,
            dma((np_,)),
            dma((np_,)),
            dma((3,)),
        ],
        compiler_params=pltpu.CompilerParams(
            collective_id=0, has_side_effects=True, vmem_limit_bytes=44 * 2**20
        ),
        cost_estimate=pl.CostEstimate(
            flops=flops, bytes_accessed=4 * rows * cols, transcendentals=0
        ),
    )(block)
    tall, tiles = rows // 2, cols // NB
    return pl.pallas_call(
        update_kernel,
        grid=(rows // tall, tiles),
        out_shape=(
            jax.ShapeDtypeStruct((NB, cols), F32),
            jax.ShapeDtypeStruct((rows, cols), F32),
        ),
        in_specs=[vmem] * 4,
        out_specs=(
            pl.BlockSpec((NB, NB), lambda i, c: (0, jnp.where(i == 0, c, tiles - 1))),
            pl.BlockSpec((tall, NB), lambda i, c: (i, c)),
        ),
        scratch_shapes=[
            pltpu.VMEM((tall, NB), F32),
            pltpu.VMEM((tall, 3 * NB), jnp.bfloat16),
            pltpu.VMEM((tiles, 3 * NB, NB), jnp.bfloat16),
        ],
        compiler_params=pltpu.CompilerParams(vmem_limit_bytes=44 * 2**20),
        cost_estimate=pl.CostEstimate(
            flops=flops, bytes_accessed=8 * rows * cols, transcendentals=0
        ),
    )(block, panel, linv, prod)


def solution(mesh):
    return jax.shard_map(
        functools.partial(body, mesh.shape["prow"], mesh.shape["pcol"]),
        mesh=mesh,
        in_specs=(P("prow", "pcol"),),
        out_specs=(P(None, "pcol"), P("prow", "pcol")),
        check_vma=False,
    )
```

```python
import functools

import jax
import jax.numpy as jnp
from jax import lax
from jax.experimental import pallas as pl
from jax.experimental.pallas import tpu as pltpu
from jax.sharding import PartitionSpec as P

NB = 256
HALF = 128
ROWS = 256
PIECE = 128
DIAG = 64
HIGHEST = lax.Precision.HIGHEST
F32 = jnp.float32


def split(x):
    hi = x.astype(jnp.bfloat16)
    return hi, (x - hi.astype(F32)).astype(jnp.bfloat16)


def left_terms(x):
    hi, lo = split(x)
    return jnp.concatenate([hi, lo, hi], axis=1)


def right_terms(x):
    hi, lo = split(x)
    return jnp.concatenate([hi, hi, lo], axis=0)


def dot3(a, b):
    return jnp.dot(a, b, preferred_element_type=F32)


def inverse_factor(square):
    n = square.shape[0]
    below = lax.broadcasted_iota(jnp.int32, (8, 1), 0)
    eye = (
        lax.broadcasted_iota(jnp.int32, (n, n), 0)
        == lax.broadcasted_iota(jnp.int32, (n, n), 1)
    ).astype(F32)
    rest = jnp.concatenate([square, eye], axis=1)
    done = []
    for g in range(0, n, 8):
        cols = [jnp.broadcast_to(rest[:, k : k + 1], rest.shape) for k in range(g, g + 8)]
        head, rest = rest[:8], rest[8:]
        for j in range(8):
            inv = 1.0 / cols[j][j : j + 1, :]
            row = head[j : j + 1, :] * inv
            if j < 7:
                head = head - jnp.where(below > j, cols[j][:8], 0.0) * row
            if g + 8 < n:
                rest = rest - cols[j][8:] * row
            for i in range(j + 1, 8):
                cols[i] = cols[i] - cols[j] * (cols[i][j : j + 1, :] * inv)
        done.append(head)
    m = jnp.concatenate(done, axis=0)
    pivots = jnp.sum(m[:, :n] * eye, axis=1, keepdims=True)
    return m[:, n:] / jnp.sqrt(pivots)


def inverse_cholesky(work):
    row_id = lax.broadcasted_iota(jnp.int32, (NB, 1), 0)

    @pl.loop(0, NB // DIAG)
    def _(b):
        at = pl.ds(pl.multiple_of(b * DIAG, DIAG), DIAG)
        band = work[at, :]
        square = band[:, :DIAG]
        for other in range(1, NB // DIAG):
            square = jnp.where(b == other, band[:, other * DIAG : (other + 1) * DIAG], square)
        new = jnp.dot(
            inverse_factor(square), band, precision=HIGHEST, preferred_element_type=F32
        )
        lower = jnp.where(row_id >= (b + 1) * DIAG, new[:, :NB].T, 0.0)
        work[...] -= jnp.dot(lower, new, precision=HIGHEST, preferred_element_type=F32)
        work[at, :] = new


def gather_kernel(
    np_, nq, block, blk, panel, linv, prod,
    acc, pair, parts, gram, gparts, gfull, work,
    load_sem, blk_sem, csend, crecv, gsend, grecv, hsend, hrecv,
    tsend, trecv, psend, precv, asend, arecv, bsend, brecv, zsend, zrecv, lsend, lrecv,
):
    p = lax.axis_index("prow")
    q = lax.axis_index("pcol")
    rows, cols = blk.shape
    steps = rows // ROWS
    pieces = rows // PIECE
    per_step = ROWS // PIECE
    ahead = pieces + pieces // 2
    first = q == 0
    inner = q > 0
    sends_on = q < nq - 1
    gs = NB // np_
    ps = HALF // np_
    pairs = np_ // 2
    parity, own_pair = lax.rem(p, 2), p // 2
    sibling = p + 1 - 2 * parity
    side = HALF // 2

    def remote(src, dst, send, recv, pp, qq):
        return pltpu.make_async_remote_copy(
            src_ref=src, dst_ref=dst, send_sem=send, recv_sem=recv,
            device_id={"prow": pp, "pcol": qq}, device_id_type=pl.DeviceIdType.MESH,
        )

    def peer(d):
        return lax.rem(p + d, np_)

    def load(h, r):
        at = pl.ds(r * PIECE, PIECE)
        return pltpu.make_async_copy(
            block.at[at, pl.ds(h * HALF, HALF)], panel.at[h, at], load_sem.at[h * pieces + r]
        )

    def load_blk(r):
        at = pl.ds(r * ROWS, ROWS)
        return pltpu.make_async_copy(block.at[at], blk.at[at], blk_sem.at[r])

    def pass_on(h, r):
        at = pl.ds(r * PIECE, PIECE)
        c = h * pieces + r
        return remote(panel.at[h, at], panel.at[h, at], csend.at[c], crecv.at[c], p, q + 1)

    def gram_part(d):
        j = peer(d)
        return remote(
            gram.at[pl.ds(pl.multiple_of(j * gs, 8), gs)], gparts.at[p],
            gsend.at[d], grecv.at[p], j, q,
        )

    def gram_wait(d):
        j = peer(d)
        return remote(
            gram.at[pl.ds(0, gs)], gparts.at[j], gsend.at[d], grecv.at[j], j, q
        )

    def spread_rows(ref, size, send, recv, d):
        at = pl.ds(pl.multiple_of(p * size, 8), size)
        return remote(ref.at[at], ref.at[at], send.at[d], recv.at[p], peer(d), q)

    def spread_wait(ref, size, send, recv, d):
        j = peer(d)
        at = pl.ds(pl.multiple_of(j * size, 8), size)
        return remote(ref.at[at], ref.at[at], send.at[d], recv.at[j], j, q)

    def rows_of(par, m):
        return pl.ds(pl.multiple_of(par * side + m * ps, 8), ps)

    def pair_part(h):
        theirs = pl.ds(pl.multiple_of((1 - parity) * side, 8), side)
        return remote(acc.at[h, theirs], pair.at[h], tsend.at[h], trecv.at[h], sibling, q)

    def other_pair(e):
        return lax.rem(own_pair + e, pairs)

    def prod_part(h, e):
        m = other_pair(e)
        return remote(
            acc.at[h, rows_of(parity, m)], parts.at[h, own_pair],
            psend.at[h, e], precv.at[h, own_pair], 2 * m + parity, q,
        )

    def prod_wait(h, e):
        m = other_pair(e)
        return remote(
            acc.at[h, rows_of(parity, m)], parts.at[h, m],
            psend.at[h, e], precv.at[h, m], 2 * m + parity, q,
        )

    def sum_part(h, e):
        m, at = other_pair(e), rows_of(parity, own_pair)
        return remote(
            prod.at[h, at], prod.at[h, at],
            asend.at[h, e], arecv.at[h, own_pair], 2 * m + parity, q,
        )

    def sum_wait(h, e):
        m = other_pair(e)
        at = rows_of(parity, m)
        return remote(
            prod.at[h, at], prod.at[h, at], asend.at[h, e], arecv.at[h, m], 2 * m + parity, q
        )

    def across_part(h, e):
        m = other_pair(e)
        at = rows_of(parity, m)
        return remote(prod.at[h, at], prod.at[h, at], bsend.at[h, e], brecv.at[h, m], sibling, q)

    def across_wait(h, e):
        m = other_pair(e)
        at = rows_of(1 - parity, m)
        return remote(prod.at[h, at], prod.at[h, at], bsend.at[h, e], brecv.at[h, m], sibling, q)

    own_l = pl.ds(pl.multiple_of(p * gs, 8), gs)

    def linv_on():
        return remote(linv.at[own_l], linv.at[own_l], zsend, zrecv, p, q + 1)

    @pl.when(first)
    def _():
        for h in range(2):
            for r in range(pieces):
                load(h, r).start()

    for r in range(steps):
        load_blk(r).start()

    barrier = pltpu.get_barrier_semaphore()
    for d in range(1, np_):
        pl.semaphore_signal(
            barrier, inc=1, device_id={"prow": peer(d), "pcol": q},
            device_id_type=pl.DeviceIdType.MESH,
        )

    @pl.when(inner)
    def _():
        pl.semaphore_signal(
            barrier, inc=1, device_id={"prow": p, "pcol": q - 1},
            device_id_type=pl.DeviceIdType.MESH,
        )

    @pl.when(sends_on)
    def _():
        pl.semaphore_signal(
            barrier, inc=1, device_id={"prow": p, "pcol": q + 1},
            device_id_type=pl.DeviceIdType.MESH,
        )

    pl.semaphore_wait(
        barrier, np_ - 1 + jnp.where(inner, 1, 0) + jnp.where(sends_on, 1, 0)
    )

    @pl.when(first)
    def _():
        for h in range(2):
            for r in range(pieces):
                load(h, r).wait()
                if nq > 1 and h * pieces + r < ahead:
                    pass_on(h, r).start()
        gram[...] = jnp.zeros_like(gram)

        @pl.loop(0, steps)
        def _(r):
            at = pl.ds(pl.multiple_of(r * ROWS, ROWS), ROWS)
            both = jnp.concatenate([panel[0, at, :], panel[1, at, :]], axis=1)
            gram[...] += jnp.dot(both.T, both, precision=HIGHEST, preferred_element_type=F32)

        for d in range(1, np_):
            gram_part(d).start()
        total = gram[own_l, :]
        for d in range(1, np_):
            gram_wait(d).wait_recv()
            total = total + gparts[peer(d)]
        gfull[own_l, :] = total
        for d in range(1, np_):
            spread_rows(gfull, gs, hsend, hrecv, d).start()
        for d in range(1, np_):
            spread_wait(gfull, gs, hsend, hrecv, d).wait_recv()
        work[:, :NB] = gfull[...]
        work[:, NB:] = (
            lax.broadcasted_iota(jnp.int32, (NB, NB), 0)
            == lax.broadcasted_iota(jnp.int32, (NB, NB), 1)
        ).astype(F32)
        inverse_cholesky(work)
        linv[...] = work[:, NB:]
        if nq > 1:
            linv_on().start()
            for r in range(ahead - pieces, pieces):
                pass_on(1, r).start()
        for d in range(1, np_):
            gram_part(d).wait_send()
            spread_rows(gfull, gs, hsend, hrecv, d).wait_send()

    acc[...] = jnp.zeros_like(acc)

    def reduce_middle(h):
        pair_part(h).wait_recv()
        mine = pl.ds(pl.multiple_of(parity * side, 8), side)
        acc[h, mine, :] += pair[h]
        for e in range(1, pairs):
            prod_part(h, e).start()

    def reduce_end(h):
        own = rows_of(parity, own_pair)
        total = acc[h, own, :]
        for e in range(1, pairs):
            prod_wait(h, e).wait_recv()
            total = total + parts[h, other_pair(e)]
        prod[h, own, :] = total
        for e in range(1, pairs):
            sum_part(h, e).start()
        across_part(h, 0).start()

    def gather_across(h):
        for e in range(1, pairs):
            sum_wait(h, e).wait_recv()
            across_part(h, e).start()

    def linv_forward():
        @pl.when(inner)
        def _():
            linv_on().wait_recv()

            @pl.when(sends_on)
            def _():
                linv_on().start()

            for d in range(1, np_):
                spread_rows(linv, gs, lsend, lrecv, d).start()

    for h in range(2):

        @pl.loop(0, steps)
        def _(r):
            at = pl.ds(pl.multiple_of(r * ROWS, ROWS), ROWS)

            for piece in range(per_step):

                @pl.when(inner)
                def _():
                    pass_on(h, r * per_step + piece).wait_recv()

                @pl.when(jnp.logical_and(inner, sends_on))
                def _():
                    pass_on(h, r * per_step + piece).start()

            if h == 0:
                load_blk(r).wait()
            left = left_terms(panel[h, at, :].T)
            for c in range(0, cols, 256):
                right = right_terms(blk[at, c : c + 256])
                acc[h, :, c : c + 256] += dot3(left, right)

            if h == 1:

                @pl.when(r == 1)
                def _():
                    reduce_middle(0)

                @pl.when(r == steps // 2)
                def _():
                    reduce_end(0)
                    linv_forward()

                @pl.when(r == steps - 2)
                def _():
                    gather_across(0)

        pair_part(h).start()

    reduce_middle(1)
    reduce_end(1)
    gather_across(1)

    @pl.when(inner)
    def _():
        for d in range(1, np_):
            spread_wait(linv, gs, lsend, lrecv, d).wait_recv()

    for h in range(2):
        for e in range(pairs):
            across_wait(h, e).wait_recv()

    for h in range(2):
        pair_part(h).wait_send()
        for e in range(pairs):
            across_part(h, e).wait_send()
        for e in range(1, pairs):
            prod_part(h, e).wait_send()
            sum_part(h, e).wait_send()

    @pl.when(inner)
    def _():
        for d in range(1, np_):
            spread_rows(linv, gs, lsend, lrecv, d).wait_send()

    @pl.when(sends_on)
    def _():
        for h in range(2):
            for r in range(pieces):
                pass_on(h, r).wait_send()
        linv_on().wait_send()


def update_kernel(block, panel, linv, prod, top, updated, basis, left, right_top):
    i, c = pl.program_id(0), pl.program_id(1)
    tall = updated.shape[0]
    down = pl.ds(pl.multiple_of(i * tall, tall), tall)
    across = pl.ds(pl.multiple_of(c * NB, NB), NB)

    @pl.when(c == 0)
    def _():
        both = jnp.concatenate([panel[0, down, :], panel[1, down, :]], axis=1)
        basis[...] = dot3(left_terms(both), right_terms(linv[...].T))
        left[...] = left_terms(basis[...])

    @pl.when(i == 0)
    def _():
        products = jnp.concatenate([prod[0, :, across], prod[1, :, across]], axis=0)
        tile = jnp.dot(linv[...], products, precision=HIGHEST, preferred_element_type=F32)
        top[...] = tile
        right_top[c] = right_terms(tile)

    in_panel = jnp.logical_and(c == 0, lax.axis_index("pcol") == 0)

    @pl.when(in_panel)
    def _():
        updated[...] = basis[...]

    @pl.when(jnp.logical_not(in_panel))
    def _():
        updated[...] = block[down, across] - dot3(left[...], right_top[c])


def body(np_, nq, block):
    rows, cols = block.shape
    steps = rows // ROWS
    pieces = rows // PIECE
    gs = NB // np_
    ps = HALF // np_
    pairs = np_ // 2
    dma = pltpu.SemaphoreType.DMA
    vmem = pl.BlockSpec(memory_space=pltpu.VMEM)
    flops = 3 * 2 * rows * NB * cols
    block, panel, linv, prod = pl.pallas_call(
        functools.partial(gather_kernel, np_, nq),
        out_shape=(
            pltpu.VMEM((rows, cols), F32),
            pltpu.VMEM((2, rows, HALF), F32),
            pltpu.VMEM((NB, NB), F32),
            pltpu.VMEM((2, HALF, cols), F32),
        ),
        in_specs=[pl.BlockSpec(memory_space=pltpu.HBM)],
        out_specs=(vmem,) * 4,
        scratch_shapes=[
            pltpu.VMEM((2, HALF, cols), F32),
            pltpu.VMEM((2, HALF // 2, cols), F32),
            pltpu.VMEM((2, pairs, ps, cols), F32),
            pltpu.VMEM((NB, NB), F32),
            pltpu.VMEM((np_, gs, NB), F32),
            pltpu.VMEM((NB, NB), F32),
            pltpu.VMEM((NB, 2 * NB), F32),
            dma((2 * pieces,)),
            dma((steps,)),
            dma((2 * pieces,)),
            dma((2 * pieces,)),
            dma((np_,)),
            dma((np_,)),
            dma((np_,)),
            dma((np_,)),
            dma((2,)),
            dma((2,)),
            dma((2, pairs)),
            dma((2, pairs)),
            dma((2, pairs)),
            dma((2, pairs)),
            dma((2, pairs)),
            dma((2, pairs)),
            dma,
            dma,
            dma((np_,)),
            dma((np_,)),
        ],
        compiler_params=pltpu.CompilerParams(
            collective_id=0, has_side_effects=True, vmem_limit_bytes=44 * 2**20
        ),
        cost_estimate=pl.CostEstimate(
            flops=flops, bytes_accessed=4 * rows * cols, transcendentals=0
        ),
    )(block)
    tall, tiles = rows // 2, cols // NB
    return pl.pallas_call(
        update_kernel,
        grid=(rows // tall, tiles),
        out_shape=(
            jax.ShapeDtypeStruct((NB, cols), F32),
            jax.ShapeDtypeStruct((rows, cols), F32),
        ),
        in_specs=[vmem] * 4,
        out_specs=(
            pl.BlockSpec((NB, NB), lambda i, c: (0, jnp.where(i == 0, c, tiles - 1))),
            pl.BlockSpec((tall, NB), lambda i, c: (i, c)),
        ),
        scratch_shapes=[
            pltpu.VMEM((tall, NB), F32),
            pltpu.VMEM((tall, 3 * NB), jnp.bfloat16),
            pltpu.VMEM((tiles, 3 * NB, NB), jnp.bfloat16),
        ],
        compiler_params=pltpu.CompilerParams(vmem_limit_bytes=20 * 2**20),
        cost_estimate=pl.CostEstimate(
            flops=flops, bytes_accessed=8 * rows * cols, transcendentals=0
        ),
    )(block, panel, linv, prod)


def solution(mesh):
    return jax.shard_map(
        functools.partial(body, mesh.shape["prow"], mesh.shape["pcol"]),
        mesh=mesh,
        in_specs=(P("prow", "pcol"),),
        out_specs=(P(None, "pcol"), P("prow", "pcol")),
        check_vma=False,
    )
```

```python
import functools

import jax
import jax.numpy as jnp
from jax import lax
from jax.experimental import pallas as pl
from jax.experimental.pallas import tpu as pltpu
from jax.sharding import PartitionSpec as P

NB = 256
HALF = 128
ROWS = 256
PIECE = 128
DIAG = 64
HIGHEST = lax.Precision.HIGHEST
F32 = jnp.float32


def split(x):
    hi = x.astype(jnp.bfloat16)
    return hi, (x - hi.astype(F32)).astype(jnp.bfloat16)


def left_terms(x):
    hi, lo = split(x)
    return jnp.concatenate([hi, lo, hi], axis=1)


def right_terms(x):
    hi, lo = split(x)
    return jnp.concatenate([hi, hi, lo], axis=0)


def dot3(a, b):
    return jnp.dot(a, b, preferred_element_type=F32)


def inverse_factor(square):
    n = square.shape[0]
    below = lax.broadcasted_iota(jnp.int32, (8, 1), 0)
    eye = (
        lax.broadcasted_iota(jnp.int32, (n, n), 0)
        == lax.broadcasted_iota(jnp.int32, (n, n), 1)
    ).astype(F32)
    rest = jnp.concatenate([square, eye], axis=1)
    done = []
    for g in range(0, n, 8):
        cols = [jnp.broadcast_to(rest[:, k : k + 1], rest.shape) for k in range(g, g + 8)]
        head, rest = rest[:8], rest[8:]
        for j in range(8):
            inv = 1.0 / cols[j][j : j + 1, :]
            row = head[j : j + 1, :] * inv
            if j < 7:
                head = head - jnp.where(below > j, cols[j][:8], 0.0) * row
            if g + 8 < n:
                rest = rest - cols[j][8:] * row
            for i in range(j + 1, 8):
                cols[i] = cols[i] - cols[j] * (cols[i][j : j + 1, :] * inv)
        done.append(head)
    m = jnp.concatenate(done, axis=0)
    pivots = jnp.sum(m[:, :n] * eye, axis=1, keepdims=True)
    return m[:, n:] / jnp.sqrt(pivots)


def inverse_cholesky(work):
    row_id = lax.broadcasted_iota(jnp.int32, (NB, 1), 0)

    @pl.loop(0, NB // DIAG)
    def _(b):
        at = pl.ds(pl.multiple_of(b * DIAG, DIAG), DIAG)
        band = work[at, :]
        square = band[:, :DIAG]
        for other in range(1, NB // DIAG):
            square = jnp.where(b == other, band[:, other * DIAG : (other + 1) * DIAG], square)
        new = jnp.dot(
            inverse_factor(square), band, precision=HIGHEST, preferred_element_type=F32
        )
        lower = jnp.where(row_id >= (b + 1) * DIAG, new[:, :NB].T, 0.0)
        work[...] -= jnp.dot(lower, new, precision=HIGHEST, preferred_element_type=F32)
        work[at, :] = new


def gather_kernel(
    np_, nq, block, blk, basis, left_out, linv, prod,
    panel, right_inv, acc, pair, parts, gram, gparts, gfull, work,
    load_sem, blk_sem, csend, crecv, gsend, grecv, hsend, hrecv,
    tsend, trecv, psend, precv, asend, arecv, bsend, brecv, zsend, zrecv, lsend, lrecv,
):
    p = lax.axis_index("prow")
    q = lax.axis_index("pcol")
    rows, cols = blk.shape
    steps = rows // ROWS
    pieces = rows // PIECE
    per_step = ROWS // PIECE
    ahead = pieces + pieces // 2
    first = q == 0
    inner = q > 0
    sends_on = q < nq - 1
    gs = NB // np_
    ps = HALF // np_
    pairs = np_ // 2
    parity, own_pair = lax.rem(p, 2), p // 2
    sibling = p + 1 - 2 * parity
    side = HALF // 2

    def remote(src, dst, send, recv, pp, qq):
        return pltpu.make_async_remote_copy(
            src_ref=src, dst_ref=dst, send_sem=send, recv_sem=recv,
            device_id={"prow": pp, "pcol": qq}, device_id_type=pl.DeviceIdType.MESH,
        )

    def peer(d):
        return lax.rem(p + d, np_)

    def load(h, r):
        at = pl.ds(r * PIECE, PIECE)
        return pltpu.make_async_copy(
            block.at[at, pl.ds(h * HALF, HALF)], panel.at[h, at], load_sem.at[h * pieces + r]
        )

    def load_blk(r):
        at = pl.ds(r * ROWS, ROWS)
        return pltpu.make_async_copy(block.at[at], blk.at[at], blk_sem.at[r])

    def pass_on(h, r):
        at = pl.ds(r * PIECE, PIECE)
        c = h * pieces + r
        return remote(panel.at[h, at], panel.at[h, at], csend.at[c], crecv.at[c], p, q + 1)

    def gram_part(d):
        j = peer(d)
        return remote(
            gram.at[pl.ds(pl.multiple_of(j * gs, 8), gs)], gparts.at[p],
            gsend.at[d], grecv.at[p], j, q,
        )

    def gram_wait(d):
        j = peer(d)
        return remote(
            gram.at[pl.ds(0, gs)], gparts.at[j], gsend.at[d], grecv.at[j], j, q
        )

    def spread_rows(ref, size, send, recv, d):
        at = pl.ds(pl.multiple_of(p * size, 8), size)
        return remote(ref.at[at], ref.at[at], send.at[d], recv.at[p], peer(d), q)

    def spread_wait(ref, size, send, recv, d):
        j = peer(d)
        at = pl.ds(pl.multiple_of(j * size, 8), size)
        return remote(ref.at[at], ref.at[at], send.at[d], recv.at[j], j, q)

    def rows_of(par, m):
        return pl.ds(pl.multiple_of(par * side + m * ps, 8), ps)

    def pair_part(h):
        theirs = pl.ds(pl.multiple_of((1 - parity) * side, 8), side)
        return remote(acc.at[h, theirs], pair.at[h], tsend.at[h], trecv.at[h], sibling, q)

    def other_pair(e):
        return lax.rem(own_pair + e, pairs)

    def prod_part(h, e):
        m = other_pair(e)
        return remote(
            acc.at[h, rows_of(parity, m)], parts.at[h, own_pair],
            psend.at[h, e], precv.at[h, own_pair], 2 * m + parity, q,
        )

    def prod_wait(h, e):
        m = other_pair(e)
        return remote(
            acc.at[h, rows_of(parity, m)], parts.at[h, m],
            psend.at[h, e], precv.at[h, m], 2 * m + parity, q,
        )

    def sum_part(h, e):
        m, at = other_pair(e), rows_of(parity, own_pair)
        return remote(
            prod.at[h, at], prod.at[h, at],
            asend.at[h, e], arecv.at[h, own_pair], 2 * m + parity, q,
        )

    def sum_wait(h, e):
        m = other_pair(e)
        at = rows_of(parity, m)
        return remote(
            prod.at[h, at], prod.at[h, at], asend.at[h, e], arecv.at[h, m], 2 * m + parity, q
        )

    def across_part(h, e):
        m = other_pair(e)
        at = rows_of(parity, m)
        return remote(prod.at[h, at], prod.at[h, at], bsend.at[h, e], brecv.at[h, m], sibling, q)

    def across_wait(h, e):
        m = other_pair(e)
        at = rows_of(1 - parity, m)
        return remote(prod.at[h, at], prod.at[h, at], bsend.at[h, e], brecv.at[h, m], sibling, q)

    own_l = pl.ds(pl.multiple_of(p * gs, 8), gs)

    def linv_on():
        return remote(linv.at[own_l], linv.at[own_l], zsend, zrecv, p, q + 1)

    @pl.when(first)
    def _():
        for h in range(2):
            for r in range(pieces):
                load(h, r).start()

    for r in range(steps):
        load_blk(r).start()

    barrier = pltpu.get_barrier_semaphore()
    for d in range(1, np_):
        pl.semaphore_signal(
            barrier, inc=1, device_id={"prow": peer(d), "pcol": q},
            device_id_type=pl.DeviceIdType.MESH,
        )

    @pl.when(inner)
    def _():
        pl.semaphore_signal(
            barrier, inc=1, device_id={"prow": p, "pcol": q - 1},
            device_id_type=pl.DeviceIdType.MESH,
        )

    @pl.when(sends_on)
    def _():
        pl.semaphore_signal(
            barrier, inc=1, device_id={"prow": p, "pcol": q + 1},
            device_id_type=pl.DeviceIdType.MESH,
        )

    pl.semaphore_wait(
        barrier, np_ - 1 + jnp.where(inner, 1, 0) + jnp.where(sends_on, 1, 0)
    )

    @pl.when(first)
    def _():
        for h in range(2):
            for r in range(pieces):
                load(h, r).wait()
                if nq > 1 and h * pieces + r < ahead:
                    pass_on(h, r).start()
        gram[...] = jnp.zeros_like(gram)

        @pl.loop(0, steps)
        def _(r):
            at = pl.ds(pl.multiple_of(r * ROWS, ROWS), ROWS)
            both = jnp.concatenate([panel[0, at, :], panel[1, at, :]], axis=1)
            gram[...] += jnp.dot(both.T, both, precision=HIGHEST, preferred_element_type=F32)

        for d in range(1, np_):
            gram_part(d).start()
        total = gram[own_l, :]
        for d in range(1, np_):
            gram_wait(d).wait_recv()
            total = total + gparts[peer(d)]
        gfull[own_l, :] = total
        for d in range(1, np_):
            spread_rows(gfull, gs, hsend, hrecv, d).start()
        for d in range(1, np_):
            spread_wait(gfull, gs, hsend, hrecv, d).wait_recv()
        work[:, :NB] = gfull[...]
        work[:, NB:] = (
            lax.broadcasted_iota(jnp.int32, (NB, NB), 0)
            == lax.broadcasted_iota(jnp.int32, (NB, NB), 1)
        ).astype(F32)
        inverse_cholesky(work)
        linv[...] = work[:, NB:]
        if nq > 1:
            linv_on().start()
            for r in range(ahead - pieces, pieces):
                pass_on(1, r).start()
        for d in range(1, np_):
            gram_part(d).wait_send()
            spread_rows(gfull, gs, hsend, hrecv, d).wait_send()

    acc[...] = jnp.zeros_like(acc)

    def reduce_middle(h):
        pair_part(h).wait_recv()
        mine = pl.ds(pl.multiple_of(parity * side, 8), side)
        acc[h, mine, :] += pair[h]
        for e in range(1, pairs):
            prod_part(h, e).start()

    def reduce_end(h):
        own = rows_of(parity, own_pair)
        total = acc[h, own, :]
        for e in range(1, pairs):
            prod_wait(h, e).wait_recv()
            total = total + parts[h, other_pair(e)]
        prod[h, own, :] = total
        for e in range(1, pairs):
            sum_part(h, e).start()
        across_part(h, 0).start()

    def gather_across(h):
        for e in range(1, pairs):
            sum_wait(h, e).wait_recv()
            across_part(h, e).start()

    def linv_forward():
        @pl.when(inner)
        def _():
            linv_on().wait_recv()

            @pl.when(sends_on)
            def _():
                linv_on().start()

            for d in range(1, np_):
                spread_rows(linv, gs, lsend, lrecv, d).start()

    for h in range(2):

        @pl.loop(0, steps)
        def _(r):
            at = pl.ds(pl.multiple_of(r * ROWS, ROWS), ROWS)

            for piece in range(per_step):

                @pl.when(inner)
                def _():
                    pass_on(h, r * per_step + piece).wait_recv()

                @pl.when(jnp.logical_and(inner, sends_on))
                def _():
                    pass_on(h, r * per_step + piece).start()

            if h == 0:
                load_blk(r).wait()
            left = left_terms(panel[h, at, :].T)
            for c in range(0, cols, 256):
                right = right_terms(blk[at, c : c + 256])
                acc[h, :, c : c + 256] += dot3(left, right)

            if h == 1:

                @pl.when(r == 1)
                def _():
                    reduce_middle(0)

                @pl.when(r == steps // 2)
                def _():
                    reduce_end(0)
                    linv_forward()

                @pl.when(r == steps - 2)
                def _():
                    gather_across(0)

        pair_part(h).start()

    @pl.when(inner)
    def _():
        for d in range(1, np_):
            spread_wait(linv, gs, lsend, lrecv, d).wait_recv()

    right_inv[...] = right_terms(linv[...].T)

    def basis_rows(begin, end):
        @pl.loop(begin, end)
        def _(r):
            at = pl.ds(pl.multiple_of(r * ROWS, ROWS), ROWS)
            both = jnp.concatenate([panel[0, at, :], panel[1, at, :]], axis=1)
            some = dot3(left_terms(both), right_inv[...])
            basis[at, :] = some
            left_out[at, :] = left_terms(some)

    basis_rows(0, steps // 3)
    reduce_middle(1)
    basis_rows(steps // 3, 2 * steps // 3)
    reduce_end(1)
    basis_rows(2 * steps // 3, steps)
    gather_across(1)

    for h in range(2):
        for e in range(pairs):
            across_wait(h, e).wait_recv()

    for h in range(2):
        pair_part(h).wait_send()
        for e in range(pairs):
            across_part(h, e).wait_send()
        for e in range(1, pairs):
            prod_part(h, e).wait_send()
            sum_part(h, e).wait_send()

    @pl.when(inner)
    def _():
        for d in range(1, np_):
            spread_rows(linv, gs, lsend, lrecv, d).wait_send()

    @pl.when(sends_on)
    def _():
        for h in range(2):
            for r in range(pieces):
                pass_on(h, r).wait_send()
        linv_on().wait_send()


def update_kernel(block, basis, left, linv, prod, top, updated, left_inv, right_top):
    i, c = pl.program_id(0), pl.program_id(1)
    tall = updated.shape[0]
    down = pl.ds(pl.multiple_of(i * tall, tall), tall)
    across = pl.ds(pl.multiple_of(c * NB, NB), NB)

    @pl.when(jnp.logical_and(i == 0, c == 0))
    def _():
        left_inv[...] = left_terms(linv[...])

    @pl.when(i == 0)
    def _():
        products = jnp.concatenate([prod[0, :, across], prod[1, :, across]], axis=0)
        tile = dot3(left_inv[...], right_terms(products))
        top[...] = tile
        right_top[c] = right_terms(tile)

    in_panel = jnp.logical_and(c == 0, lax.axis_index("pcol") == 0)

    @pl.when(in_panel)
    def _():
        updated[...] = basis[down, :]

    @pl.when(jnp.logical_not(in_panel))
    def _():
        updated[...] = block[down, across] - dot3(left[down, :], right_top[c])


def body(np_, nq, block):
    rows, cols = block.shape
    steps = rows // ROWS
    pieces = rows // PIECE
    gs = NB // np_
    ps = HALF // np_
    pairs = np_ // 2
    dma = pltpu.SemaphoreType.DMA
    vmem = pl.BlockSpec(memory_space=pltpu.VMEM)
    flops = 3 * 2 * rows * NB * cols
    block, basis, left, linv, prod = pl.pallas_call(
        functools.partial(gather_kernel, np_, nq),
        out_shape=(
            pltpu.VMEM((rows, cols), F32),
            pltpu.VMEM((rows, NB), F32),
            pltpu.VMEM((rows, 3 * NB), jnp.bfloat16),
            pltpu.VMEM((NB, NB), F32),
            pltpu.VMEM((2, HALF, cols), F32),
        ),
        in_specs=[pl.BlockSpec(memory_space=pltpu.HBM)],
        out_specs=(vmem,) * 5,
        scratch_shapes=[
            pltpu.VMEM((2, rows, HALF), F32),
            pltpu.VMEM((3 * NB, NB), jnp.bfloat16),
            pltpu.VMEM((2, HALF, cols), F32),
            pltpu.VMEM((2, HALF // 2, cols), F32),
            pltpu.VMEM((2, pairs, ps, cols), F32),
            pltpu.VMEM((NB, NB), F32),
            pltpu.VMEM((np_, gs, NB), F32),
            pltpu.VMEM((NB, NB), F32),
            pltpu.VMEM((NB, 2 * NB), F32),
            dma((2 * pieces,)),
            dma((steps,)),
            dma((2 * pieces,)),
            dma((2 * pieces,)),
            dma((np_,)),
            dma((np_,)),
            dma((np_,)),
            dma((np_,)),
            dma((2,)),
            dma((2,)),
            dma((2, pairs)),
            dma((2, pairs)),
            dma((2, pairs)),
            dma((2, pairs)),
            dma((2, pairs)),
            dma((2, pairs)),
            dma,
            dma,
            dma((np_,)),
            dma((np_,)),
        ],
        compiler_params=pltpu.CompilerParams(
            collective_id=0, has_side_effects=True, vmem_limit_bytes=44 * 2**20
        ),
        cost_estimate=pl.CostEstimate(
            flops=flops, bytes_accessed=4 * rows * cols, transcendentals=0
        ),
    )(block)
    tall, tiles = rows // 2, cols // NB
    return pl.pallas_call(
        update_kernel,
        grid=(rows // tall, tiles),
        out_shape=(
            jax.ShapeDtypeStruct((NB, cols), F32),
            jax.ShapeDtypeStruct((rows, cols), F32),
        ),
        in_specs=[vmem] * 5,
        out_specs=(
            pl.BlockSpec((NB, NB), lambda i, c: (0, jnp.where(i == 0, c, tiles - 1))),
            pl.BlockSpec((tall, NB), lambda i, c: (i, c)),
        ),
        scratch_shapes=[
            pltpu.VMEM((NB, 3 * NB), jnp.bfloat16),
            pltpu.VMEM((tiles, 3 * NB, NB), jnp.bfloat16),
        ],
        compiler_params=pltpu.CompilerParams(vmem_limit_bytes=20 * 2**20),
        cost_estimate=pl.CostEstimate(
            flops=flops, bytes_accessed=8 * rows * cols, transcendentals=0
        ),
    )(block, basis, left, linv, prod)


def solution(mesh):
    return jax.shard_map(
        functools.partial(body, mesh.shape["prow"], mesh.shape["pcol"]),
        mesh=mesh,
        in_specs=(P("prow", "pcol"),),
        out_specs=(P(None, "pcol"), P("prow", "pcol")),
        check_vma=False,
    )
```

```python
import functools

import jax
import jax.numpy as jnp
from jax import lax
from jax.experimental import pallas as pl
from jax.experimental.pallas import tpu as pltpu
from jax.sharding import PartitionSpec as P

NB = 256
HALF = 128
ROWS = 256
PIECE = 64
DIAG = 64
HIGHEST = lax.Precision.HIGHEST
F32 = jnp.float32


def split(x):
    hi = x.astype(jnp.bfloat16)
    return hi, (x - hi.astype(F32)).astype(jnp.bfloat16)


def left_terms(x):
    hi, lo = split(x)
    return jnp.concatenate([hi, lo, hi], axis=1)


def right_terms(x):
    hi, lo = split(x)
    return jnp.concatenate([hi, hi, lo], axis=0)


def dot3(a, b):
    return jnp.dot(a, b, preferred_element_type=F32)


def inverse_factor(square):
    n = square.shape[0]
    below = lax.broadcasted_iota(jnp.int32, (8, 1), 0)
    eye = (
        lax.broadcasted_iota(jnp.int32, (n, n), 0)
        == lax.broadcasted_iota(jnp.int32, (n, n), 1)
    ).astype(F32)
    rest = jnp.concatenate([square, eye], axis=1)
    done = []
    for g in range(0, n, 8):
        cols = [jnp.broadcast_to(rest[:, k : k + 1], rest.shape) for k in range(g, g + 8)]
        head, rest = rest[:8], rest[8:]
        for j in range(8):
            inv = 1.0 / cols[j][j : j + 1, :]
            row = head[j : j + 1, :] * inv
            if j < 7:
                head = head - jnp.where(below > j, cols[j][:8], 0.0) * row
            if g + 8 < n:
                rest = rest - cols[j][8:] * row
            for i in range(j + 1, 8):
                cols[i] = cols[i] - cols[j] * (cols[i][j : j + 1, :] * inv)
        done.append(head)
    m = jnp.concatenate(done, axis=0)
    pivots = jnp.sum(m[:, :n] * eye, axis=1, keepdims=True)
    return m[:, n:] / jnp.sqrt(pivots)


def inverse_cholesky(work):
    row_id = lax.broadcasted_iota(jnp.int32, (NB, 1), 0)

    @pl.loop(0, NB // DIAG)
    def _(b):
        at = pl.ds(pl.multiple_of(b * DIAG, DIAG), DIAG)
        band = work[at, :]
        square = band[:, :DIAG]
        for other in range(1, NB // DIAG):
            square = jnp.where(b == other, band[:, other * DIAG : (other + 1) * DIAG], square)
        new = jnp.dot(
            inverse_factor(square), band, precision=HIGHEST, preferred_element_type=F32
        )
        lower = jnp.where(row_id >= (b + 1) * DIAG, new[:, :NB].T, 0.0)
        work[...] -= jnp.dot(lower, new, precision=HIGHEST, preferred_element_type=F32)
        work[at, :] = new


def gather_kernel(
    np_, nq, block, blk, basis, left_out, linv, prod,
    panel, right_inv, acc, pair, parts, gram, gparts, gfull, work,
    load_sem, blk_sem, csend, crecv, gsend, grecv, hsend, hrecv,
    tsend, trecv, psend, precv, asend, arecv, bsend, brecv, zsend, zrecv, lsend, lrecv,
):
    p = lax.axis_index("prow")
    q = lax.axis_index("pcol")
    rows, cols = blk.shape
    steps = rows // ROWS
    pieces = rows // PIECE
    per_step = ROWS // PIECE
    ahead = pieces + pieces // 2
    first = q == 0
    inner = q > 0
    sends_on = q < nq - 1
    gs = NB // np_
    ps = HALF // np_
    pairs = np_ // 2
    parity, own_pair = lax.rem(p, 2), p // 2
    sibling = p + 1 - 2 * parity
    side = HALF // 2

    def remote(src, dst, send, recv, pp, qq):
        return pltpu.make_async_remote_copy(
            src_ref=src, dst_ref=dst, send_sem=send, recv_sem=recv,
            device_id={"prow": pp, "pcol": qq}, device_id_type=pl.DeviceIdType.MESH,
        )

    def peer(d):
        return lax.rem(p + d, np_)

    def load(h, r):
        at = pl.ds(r * PIECE, PIECE)
        return pltpu.make_async_copy(
            block.at[at, pl.ds(h * HALF, HALF)], panel.at[h, at], load_sem.at[h * pieces + r]
        )

    def load_blk(r):
        at = pl.ds(r * ROWS, ROWS)
        return pltpu.make_async_copy(block.at[at], blk.at[at], blk_sem.at[r])

    def pass_on(h, r):
        at = pl.ds(r * PIECE, PIECE)
        c = h * pieces + r
        return remote(panel.at[h, at], panel.at[h, at], csend.at[c], crecv.at[c], p, q + 1)

    def gram_part(d):
        j = peer(d)
        return remote(
            gram.at[pl.ds(pl.multiple_of(j * gs, 8), gs)], gparts.at[p],
            gsend.at[d], grecv.at[p], j, q,
        )

    def gram_wait(d):
        j = peer(d)
        return remote(
            gram.at[pl.ds(0, gs)], gparts.at[j], gsend.at[d], grecv.at[j], j, q
        )

    def spread_rows(ref, size, send, recv, d):
        at = pl.ds(pl.multiple_of(p * size, 8), size)
        return remote(ref.at[at], ref.at[at], send.at[d], recv.at[p], peer(d), q)

    def spread_wait(ref, size, send, recv, d):
        j = peer(d)
        at = pl.ds(pl.multiple_of(j * size, 8), size)
        return remote(ref.at[at], ref.at[at], send.at[d], recv.at[j], j, q)

    def rows_of(par, m):
        return pl.ds(pl.multiple_of(par * side + m * ps, 8), ps)

    def pair_part(h):
        theirs = pl.ds(pl.multiple_of((1 - parity) * side, 8), side)
        return remote(acc.at[h, theirs], pair.at[h], tsend.at[h], trecv.at[h], sibling, q)

    def other_pair(e):
        return lax.rem(own_pair + e, pairs)

    def prod_part(h, e):
        m = other_pair(e)
        return remote(
            acc.at[h, rows_of(parity, m)], parts.at[h, own_pair],
            psend.at[h, e], precv.at[h, own_pair], 2 * m + parity, q,
        )

    def prod_wait(h, e):
        m = other_pair(e)
        return remote(
            acc.at[h, rows_of(parity, m)], parts.at[h, m],
            psend.at[h, e], precv.at[h, m], 2 * m + parity, q,
        )

    def sum_part(h, e):
        m, at = other_pair(e), rows_of(parity, own_pair)
        return remote(
            prod.at[h, at], prod.at[h, at],
            asend.at[h, e], arecv.at[h, own_pair], 2 * m + parity, q,
        )

    def sum_wait(h, e):
        m = other_pair(e)
        at = rows_of(parity, m)
        return remote(
            prod.at[h, at], prod.at[h, at], asend.at[h, e], arecv.at[h, m], 2 * m + parity, q
        )

    def across_part(h, e):
        m = other_pair(e)
        at = rows_of(parity, m)
        return remote(prod.at[h, at], prod.at[h, at], bsend.at[h, e], brecv.at[h, m], sibling, q)

    def across_wait(h, e):
        m = other_pair(e)
        at = rows_of(1 - parity, m)
        return remote(prod.at[h, at], prod.at[h, at], bsend.at[h, e], brecv.at[h, m], sibling, q)

    own_l = pl.ds(pl.multiple_of(p * gs, 8), gs)

    def linv_on():
        return remote(linv.at[own_l], linv.at[own_l], zsend, zrecv, p, q + 1)

    @pl.when(first)
    def _():
        for h in range(2):
            for r in range(pieces):
                load(h, r).start()

    for r in range(steps):
        load_blk(r).start()

    barrier = pltpu.get_barrier_semaphore()
    for d in range(1, np_):
        pl.semaphore_signal(
            barrier, inc=1, device_id={"prow": peer(d), "pcol": q},
            device_id_type=pl.DeviceIdType.MESH,
        )

    @pl.when(inner)
    def _():
        pl.semaphore_signal(
            barrier, inc=1, device_id={"prow": p, "pcol": q - 1},
            device_id_type=pl.DeviceIdType.MESH,
        )

    @pl.when(sends_on)
    def _():
        pl.semaphore_signal(
            barrier, inc=1, device_id={"prow": p, "pcol": q + 1},
            device_id_type=pl.DeviceIdType.MESH,
        )

    pl.semaphore_wait(
        barrier, np_ - 1 + jnp.where(inner, 1, 0) + jnp.where(sends_on, 1, 0)
    )

    @pl.when(first)
    def _():
        for h in range(2):
            for r in range(pieces):
                load(h, r).wait()
                if nq > 1 and h * pieces + r < ahead:
                    pass_on(h, r).start()
        gram[...] = jnp.zeros_like(gram)

        @pl.loop(0, steps)
        def _(r):
            at = pl.ds(pl.multiple_of(r * ROWS, ROWS), ROWS)
            both = jnp.concatenate([panel[0, at, :], panel[1, at, :]], axis=1)
            gram[...] += jnp.dot(both.T, both, precision=HIGHEST, preferred_element_type=F32)

        for d in range(1, np_):
            gram_part(d).start()
        total = gram[own_l, :]
        for d in range(1, np_):
            gram_wait(d).wait_recv()
            total = total + gparts[peer(d)]
        gfull[own_l, :] = total
        for d in range(1, np_):
            spread_rows(gfull, gs, hsend, hrecv, d).start()
        for d in range(1, np_):
            spread_wait(gfull, gs, hsend, hrecv, d).wait_recv()
        work[:, :NB] = gfull[...]
        work[:, NB:] = (
            lax.broadcasted_iota(jnp.int32, (NB, NB), 0)
            == lax.broadcasted_iota(jnp.int32, (NB, NB), 1)
        ).astype(F32)
        inverse_cholesky(work)
        linv[...] = work[:, NB:]
        if nq > 1:
            linv_on().start()
            for r in range(ahead - pieces, pieces):
                pass_on(1, r).start()
        for d in range(1, np_):
            gram_part(d).wait_send()
            spread_rows(gfull, gs, hsend, hrecv, d).wait_send()

    acc[...] = jnp.zeros_like(acc)

    def reduce_middle(h):
        pair_part(h).wait_recv()
        mine = pl.ds(pl.multiple_of(parity * side, 8), side)
        acc[h, mine, :] += pair[h]
        for e in range(1, pairs):
            prod_part(h, e).start()

    def reduce_end(h):
        own = rows_of(parity, own_pair)
        total = acc[h, own, :]
        for e in range(1, pairs):
            prod_wait(h, e).wait_recv()
            total = total + parts[h, other_pair(e)]
        prod[h, own, :] = total
        for e in range(1, pairs):
            sum_part(h, e).start()
        across_part(h, 0).start()

    def gather_across(h):
        for e in range(1, pairs):
            sum_wait(h, e).wait_recv()
            across_part(h, e).start()

    def linv_forward():
        @pl.when(inner)
        def _():
            linv_on().wait_recv()

            @pl.when(sends_on)
            def _():
                linv_on().start()

            for d in range(1, np_):
                spread_rows(linv, gs, lsend, lrecv, d).start()

    for h in range(2):

        @pl.loop(0, steps)
        def _(r):
            at = pl.ds(pl.multiple_of(r * ROWS, ROWS), ROWS)

            for piece in range(per_step):

                @pl.when(inner)
                def _():
                    pass_on(h, r * per_step + piece).wait_recv()

                @pl.when(jnp.logical_and(inner, sends_on))
                def _():
                    pass_on(h, r * per_step + piece).start()

            if h == 0:
                load_blk(r).wait()
            left = left_terms(panel[h, at, :].T)
            for c in range(0, cols, 256):
                right = right_terms(blk[at, c : c + 256])
                acc[h, :, c : c + 256] += dot3(left, right)

            if h == 1:

                @pl.when(r == 1)
                def _():
                    reduce_middle(0)

                @pl.when(r == steps // 2)
                def _():
                    reduce_end(0)
                    linv_forward()

                @pl.when(r == steps - 2)
                def _():
                    gather_across(0)

        pair_part(h).start()

    @pl.when(inner)
    def _():
        for d in range(1, np_):
            spread_wait(linv, gs, lsend, lrecv, d).wait_recv()

    right_inv[...] = right_terms(linv[...].T)

    def basis_rows(begin, end):
        @pl.loop(begin, end)
        def _(r):
            at = pl.ds(pl.multiple_of(r * ROWS, ROWS), ROWS)
            both = jnp.concatenate([panel[0, at, :], panel[1, at, :]], axis=1)
            some = dot3(left_terms(both), right_inv[...])
            basis[at, :] = some
            left_out[at, :] = left_terms(some)

    basis_rows(0, steps // 3)
    reduce_middle(1)
    basis_rows(steps // 3, 2 * steps // 3)
    reduce_end(1)
    basis_rows(2 * steps // 3, steps)
    gather_across(1)

    for h in range(2):
        for e in range(pairs):
            across_wait(h, e).wait_recv()

    for h in range(2):
        pair_part(h).wait_send()
        for e in range(pairs):
            across_part(h, e).wait_send()
        for e in range(1, pairs):
            prod_part(h, e).wait_send()
            sum_part(h, e).wait_send()

    @pl.when(inner)
    def _():
        for d in range(1, np_):
            spread_rows(linv, gs, lsend, lrecv, d).wait_send()

    @pl.when(sends_on)
    def _():
        for h in range(2):
            for r in range(pieces):
                pass_on(h, r).wait_send()
        linv_on().wait_send()


def update_kernel(block, basis, left, linv, prod, top, updated, left_inv, right_top):
    i, c = pl.program_id(0), pl.program_id(1)
    tall = updated.shape[0]
    down = pl.ds(pl.multiple_of(i * tall, tall), tall)
    across = pl.ds(pl.multiple_of(c * NB, NB), NB)

    @pl.when(jnp.logical_and(i == 0, c == 0))
    def _():
        left_inv[...] = left_terms(linv[...])

    @pl.when(i == 0)
    def _():
        products = jnp.concatenate([prod[0, :, across], prod[1, :, across]], axis=0)
        tile = dot3(left_inv[...], right_terms(products))
        top[...] = tile
        right_top[c] = right_terms(tile)

    in_panel = jnp.logical_and(c == 0, lax.axis_index("pcol") == 0)

    @pl.when(in_panel)
    def _():
        updated[...] = basis[down, :]

    @pl.when(jnp.logical_not(in_panel))
    def _():
        updated[...] = block[down, across] - dot3(left[down, :], right_top[c])


def body(np_, nq, block):
    rows, cols = block.shape
    steps = rows // ROWS
    pieces = rows // PIECE
    gs = NB // np_
    ps = HALF // np_
    pairs = np_ // 2
    dma = pltpu.SemaphoreType.DMA
    vmem = pl.BlockSpec(memory_space=pltpu.VMEM)
    flops = 3 * 2 * rows * NB * cols
    block, basis, left, linv, prod = pl.pallas_call(
        functools.partial(gather_kernel, np_, nq),
        out_shape=(
            pltpu.VMEM((rows, cols), F32),
            pltpu.VMEM((rows, NB), F32),
            pltpu.VMEM((rows, 3 * NB), jnp.bfloat16),
            pltpu.VMEM((NB, NB), F32),
            pltpu.VMEM((2, HALF, cols), F32),
        ),
        in_specs=[pl.BlockSpec(memory_space=pltpu.HBM)],
        out_specs=(vmem,) * 5,
        scratch_shapes=[
            pltpu.VMEM((2, rows, HALF), F32),
            pltpu.VMEM((3 * NB, NB), jnp.bfloat16),
            pltpu.VMEM((2, HALF, cols), F32),
            pltpu.VMEM((2, HALF // 2, cols), F32),
            pltpu.VMEM((2, pairs, ps, cols), F32),
            pltpu.VMEM((NB, NB), F32),
            pltpu.VMEM((np_, gs, NB), F32),
            pltpu.VMEM((NB, NB), F32),
            pltpu.VMEM((NB, 2 * NB), F32),
            dma((2 * pieces,)),
            dma((steps,)),
            dma((2 * pieces,)),
            dma((2 * pieces,)),
            dma((np_,)),
            dma((np_,)),
            dma((np_,)),
            dma((np_,)),
            dma((2,)),
            dma((2,)),
            dma((2, pairs)),
            dma((2, pairs)),
            dma((2, pairs)),
            dma((2, pairs)),
            dma((2, pairs)),
            dma((2, pairs)),
            dma,
            dma,
            dma((np_,)),
            dma((np_,)),
        ],
        compiler_params=pltpu.CompilerParams(
            collective_id=0, has_side_effects=True, vmem_limit_bytes=44 * 2**20
        ),
        cost_estimate=pl.CostEstimate(
            flops=flops, bytes_accessed=4 * rows * cols, transcendentals=0
        ),
    )(block)
    tall, tiles = rows // 2, cols // NB
    return pl.pallas_call(
        update_kernel,
        grid=(rows // tall, tiles),
        out_shape=(
            jax.ShapeDtypeStruct((NB, cols), F32),
            jax.ShapeDtypeStruct((rows, cols), F32),
        ),
        in_specs=[vmem] * 5,
        out_specs=(
            pl.BlockSpec((NB, NB), lambda i, c: (0, jnp.where(i == 0, c, tiles - 1))),
            pl.BlockSpec((tall, NB), lambda i, c: (i, c)),
        ),
        scratch_shapes=[
            pltpu.VMEM((NB, 3 * NB), jnp.bfloat16),
            pltpu.VMEM((tiles, 3 * NB, NB), jnp.bfloat16),
        ],
        compiler_params=pltpu.CompilerParams(vmem_limit_bytes=20 * 2**20),
        cost_estimate=pl.CostEstimate(
            flops=flops, bytes_accessed=8 * rows * cols, transcendentals=0
        ),
    )(block, basis, left, linv, prod)


def solution(mesh):
    return jax.shard_map(
        functools.partial(body, mesh.shape["prow"], mesh.shape["pcol"]),
        mesh=mesh,
        in_specs=(P("prow", "pcol"),),
        out_specs=(P(None, "pcol"), P("prow", "pcol")),
        check_vma=False,
    )
```
